128 devices in a mesh: ctx: 16 (over z, x), tp: 8 (over y, core).
Axes of the slice: x: 4, y: 4, z: 4, core: 2. Of those that a mesh axis runs over, the one named last changes fastest.
Arguments:
- inputs: bfloat16 [8192, 16384], P('ctx', 'tp'), may hold values from -6 to 6
- gate_input: bfloat16 [8192, 16384], P('ctx', 'tp'), may hold values from -120 to 120
- step_size: float32 [256, 8192], P('tp', 'ctx'), may hold values from 0 to 1, as said below
- input_map: bfloat16 [8192, 2048], P('ctx', 'tp'), may hold values from -6 to 6
- output_map: bfloat16 [8192, 2048], P('ctx', 'tp'), may hold values from -6 to 6
- decay_rate: float32 [256], P('tp'), may hold values from 1 to 4
- skip_weight: float32 [256], P('tp'), may hold values from 0.5 to 1.5
- norm_gain: float32 [16384], P('tp'), may hold values from 0.1 to 1.9
- out_grad: bfloat16 [8192, 16384], P('ctx', 'tp'), may hold values from -6 to 6
Outputs:
- normed: bfloat16 [8192, 16384], P('ctx', 'tp')
- grad_inputs: bfloat16 [8192, 16384], P('ctx', 'tp')
- grad_gate: bfloat16 [8192, 16384], P('ctx', 'tp')
- grad_input_map: bfloat16 [8192, 2048], P('ctx', 'tp')
- grad_output_map: bfloat16 [8192, 2048], P('ctx', 'tp')
The draws below stay inside these ranges and needn't reach their ends.
Inputs may be any that keep to these rules, and one draw needn't show every extreme that they name: `step_size`: positive.
All inputs are finite; a program needn't handle non-finite values.
Results may differ from the reference program's by a relative error of at most 0.015.
Values may be sent and summed in bfloat16 or wider, within the bound.
No kernel may reach another device: no remote copies, remote signals or barrier semaphores. Data moves between devices by JAX's collectives and lax.ppermute only.
A program may use at most 192 MiB of HBM per device.

```python
import math
import jax
import jax.numpy as jnp
from jax import lax

H = 256
P_SIZE = 64
N = 256
G = 8
BLOCK = 256
TOK_DEV = 512
TOKENS = 8192
N_CTX = 16


def decay_values(key):
    uniform_part = jax.random.uniform(jax.random.fold_in(key, 101), (H,), jnp.float32)
    return 4.0 ** uniform_part


def draw_decay_rate(key, part):
    return decay_values(key).astype(jnp.float32)


def draw_step_size(key, part):
    decay_rates = decay_values(key)
    key = jax.random.fold_in(key, 7)
    keys_list = jax.random.split(key, 7)
    share = 0.5
    fast = jax.random.uniform(keys_list[0], (H,), jnp.float32) < share
    slow_total = jax.random.uniform(keys_list[1], (H,), jnp.float32, 0.2, 0.6)
    fast_len = jax.random.uniform(keys_list[2], (H,), jnp.float32, 30.0, 50.0)
    per_step = jnp.where(fast, 1.0 / fast_len, slow_total / TOKENS)
    rough = jax.random.uniform(keys_list[3], (H, TOKENS), jnp.float32, 0.5, 1.5)
    seg_factor = jnp.exp(jax.random.uniform(keys_list[4], (H, TOKENS // TOK_DEV, 1), jnp.float32, math.log(0.6), math.log(1.5)))
    seg_factor = jnp.broadcast_to(seg_factor, (H, TOKENS // TOK_DEV, TOK_DEV)).reshape(H, TOKENS)
    baseline_step = per_step[:, None] / decay_rates[:, None] * rough * seg_factor
    spots = jax.random.randint(keys_list[5], (H, 3), 0, TOKENS)
    loss_values = jax.random.uniform(keys_list[6], (H, 3), jnp.float32, 0.2, 0.35)
    spike_amount = -jnp.log(1.0 - loss_values) / decay_rates[:, None]
    match_count = jnp.arange(TOKENS)[None, :, None] == spots[:, None, :]
    spike_position = jnp.sum(jnp.where(match_count, spike_amount[:, None, :], 0.0), axis=2)
    return jnp.where(jnp.any(match_count, axis=2), spike_position, baseline_step).astype(jnp.float32)


def draw_gate_input(key, part):
    key = jax.random.fold_in(key, 3)
    keys_list = jax.random.split(key, 3)
    columns = jnp.arange(H * P_SIZE, dtype=jnp.float32) / (H * P_SIZE)
    col_scale = 10.0 ** columns * jax.random.uniform(keys_list[1], (H * P_SIZE,), jnp.float32, 1.0, 1.5)
    row_scale = 10.0 ** jax.random.uniform(keys_list[2], (TOKENS, 1), jnp.float32)
    base_val = jnp.clip(jax.random.normal(keys_list[0], (TOKENS, H * P_SIZE), jnp.float32), -4.0, 4.0)
    return (0.1 * base_val * col_scale[None, :] * row_scale).astype(jnp.bfloat16)


def block_levels(rng, dims, cuts, smallest, top_value):
    loudness, own = 1.0, jax.random.fold_in(rng, 6)
    for dim, shards_of in cuts:
        steps = jnp.exp(jax.random.uniform(jax.random.fold_in(own, dim), (shards_of,), jnp.float32, smallest / len(cuts), top_value / len(cuts)))
        loudness = loudness * jnp.repeat(steps, dims[dim] // shards_of).reshape([-1 if axis == dim else 1 for axis in range(len(dims))])
    return loudness


def normal_values(rng, dims, spread, most, shards=(), kind=jnp.bfloat16):
    level = block_levels(rng, dims, shards, -0.22, 0.18) if shards else 1.0
    values = jax.random.normal(rng, dims, jnp.float32) * spread * level
    return jnp.minimum(jnp.maximum(values, -most), most).astype(kind)


def setup_inputs(seed: int = 0) -> dict:
    seeds = jax.random.split(jax.random.key(seed), 10)
    inputs = normal_values(seeds[0], (TOKENS, H * P_SIZE), 1.0, 6.0, ((0, 16), (1, 8)))
    gate_input = draw_gate_input(jax.random.fold_in(seeds[9], 71), 0)
    step_size = draw_step_size(jax.random.fold_in(seeds[9], 71), 0)
    input_map = normal_values(seeds[3], (TOKENS, G * N), 1.0, 6.0, ((0, 16), (1, 8)))
    output_map = normal_values(seeds[4], (TOKENS, G * N), 1.0, 6.0, ((0, 16), (1, 8)))
    decay_rate = draw_decay_rate(jax.random.fold_in(seeds[9], 71), 0)
    skip_weight = jnp.clip(0.5 + 1.0 * jax.random.uniform(seeds[6], (H,), jnp.float32) ** block_levels(seeds[6], (H,), ((0, 8),), -0.2, 0.2), 0.5, 1.5)
    norm_gain = jnp.clip(1.0 + 0.18 * jax.random.normal(seeds[7], (H * P_SIZE,), jnp.float32), 0.1, 1.9)
    out_grad = normal_values(seeds[8], (TOKENS, H * P_SIZE), 1.0, 6.0, ((0, 16), (1, 8)))
    return dict(inputs=inputs, gate_input=gate_input, step_size=step_size, input_map=input_map, output_map=output_map, decay_rate=decay_rate, skip_weight=skip_weight, norm_gain=norm_gain, out_grad=out_grad)


EPS = 1e-05

def decay_logs(step_size, decay_rate):
    return -decay_rate[:, None] * step_size

def segment_map(inputs, gate_input, step_size, input_map, output_map, decay_rate, skip_weight, state_in):
    length = inputs.shape[0]
    head_count = step_size.shape[0]
    groups = input_map.shape[1] // N
    per_group = head_count // groups
    blocks = length // BLOCK
    log_decay = decay_logs(step_size, decay_rate).reshape(head_count, blocks, BLOCK)
    inner_cum = jnp.cumsum(log_decay, axis=2)
    cum_heads = inner_cum.reshape(groups, per_group, blocks, BLOCK)
    total_heads = inner_cum[:, :, -1].reshape(groups, per_group, blocks)
    values = inputs.reshape(blocks, BLOCK, groups, per_group, P_SIZE)
    keys_in = input_map.reshape(blocks, BLOCK, groups, N)
    queries = output_map.reshape(blocks, BLOCK, groups, N)
    steps_blk = step_size.reshape(groups, per_group, blocks, BLOCK)
    scores = jnp.einsum('bqgn,bsgn->bgqs', queries, keys_in, preferred_element_type=jnp.float32)
    lower_mask = jnp.arange(BLOCK)[:, None] >= jnp.arange(BLOCK)[None, :]
    cum_order = cum_heads.transpose(2, 0, 1, 3)
    decay_gap = jnp.where(lower_mask, cum_order[..., :, None] - cum_order[..., None, :], 0.0)
    step_order = steps_blk.transpose(2, 0, 1, 3)
    weights = jnp.where(lower_mask, jnp.exp(decay_gap), 0.0) * scores[:, :, None] * step_order[..., None, :]
    weights = weights.astype(jnp.bfloat16)
    within = jnp.einsum('bghqs,bsghp->bqghp', weights, values, preferred_element_type=jnp.float32)
    end_weight = (jnp.exp(cum_heads[..., -1:] - cum_heads) * steps_blk).transpose(2, 3, 0, 1)
    scaled_keys = (keys_in[:, :, :, None, :] * end_weight[..., None]).astype(jnp.bfloat16)
    block_states = jnp.einsum('bsghp,bsghn->bghpn', values, scaled_keys, preferred_element_type=jnp.float32)
    running = state_in.reshape(groups, per_group, P_SIZE, N)
    inter_list = []
    for block_id in range(blocks):
        inter_list.append(jnp.einsum('qgn,ghpn->qghp', queries[block_id].astype(jnp.float32), running, precision=lax.Precision.HIGHEST))
        running = jnp.exp(total_heads[:, :, block_id])[:, :, None, None] * running + block_states[block_id]
    carried = jnp.stack(inter_list) * jnp.exp(cum_heads).transpose(2, 3, 0, 1)[..., None]
    skip_heads = skip_weight.reshape(groups, per_group)[:, :, None]
    mixed_out = within + carried + skip_heads * values.astype(jnp.float32)
    gate_wide = gate_input.reshape(blocks, BLOCK, groups, per_group, P_SIZE).astype(jnp.float32)
    gated_out = mixed_out * jax.nn.silu(gate_wide)
    return (gated_out.reshape(length, head_count * P_SIZE), running.reshape(head_count, P_SIZE, N))

def segment_pass(packed, state_in, decay_rate, skip_weight, norm_gain):
    inputs, gate_input, step_size, input_map, output_map, out_grad = packed

    def local_fn(values_in, gate_in, keys_map, query_map):
        return segment_map(values_in, gate_in, step_size, keys_map, query_map, decay_rate, skip_weight, state_in)
    (gated_out, final_state), pullback = jax.vjp(local_fn, inputs, gate_input, input_map, output_map)
    full_width = H * P_SIZE
    squares = lax.optimization_barrier(jnp.sum(gated_out * gated_out, axis=1))
    inv_rms = lax.rsqrt(squares / full_width + EPS)
    normed = (gated_out * inv_rms[:, None] * norm_gain).astype(jnp.bfloat16)
    scaled_grad = norm_gain * out_grad.astype(jnp.float32)
    product = lax.optimization_barrier(jnp.sum(gated_out * scaled_grad, axis=1))
    grad_gated = inv_rms[:, None] * scaled_grad - gated_out * (inv_rms ** 3 * product / full_width)[:, None]
    length = inputs.shape[0]
    head_count = step_size.shape[0]
    groups = input_map.shape[1] // N
    per_group = head_count // groups
    grad_mixed = grad_gated * jax.nn.silu(gate_input.astype(jnp.float32))
    seg_cum = jnp.exp(jnp.cumsum(decay_logs(step_size, decay_rate), axis=1)).T.reshape(length, groups, per_group)
    weighted = grad_mixed.reshape(length, groups, per_group, P_SIZE) * seg_cum[..., None]
    local_grad = jnp.einsum('tghp,tgn->ghpn', weighted, output_map.reshape(length, groups, N).astype(jnp.float32), precision=lax.Precision.HIGHEST).reshape(head_count, P_SIZE, N).astype(jnp.bfloat16)
    local_grad = lax.optimization_barrier(local_grad)
    return (normed, local_grad, grad_gated, pullback)

def reference(inputs, gate_input, step_size, input_map, output_map, decay_rate, skip_weight, norm_gain, out_grad):
    seg_count = N_CTX
    seg_len = TOK_DEV

    def by_rows(array):
        return array.reshape(seg_count, seg_len, array.shape[1])
    packed_all = (by_rows(inputs), by_rows(gate_input), step_size.reshape(H, seg_count, seg_len).transpose(1, 0, 2), by_rows(input_map), by_rows(output_map), by_rows(out_grad))
    zero_state = jnp.zeros((H, P_SIZE, N), jnp.float32)

    def end_state(packed):
        seg_inputs, seg_gate, seg_step, seg_keys, seg_queries, seg_grad = packed
        ends = segment_map(seg_inputs, seg_gate, seg_step, seg_keys, seg_queries, decay_rate, skip_weight, zero_state)[1].astype(jnp.bfloat16)
        decays = jnp.exp(lax.optimization_barrier(jnp.sum(decay_logs(seg_step, decay_rate), axis=1))).astype(jnp.bfloat16)
        return lax.optimization_barrier((ends, decays))
    all_ends, all_decays = lax.map(end_state, packed_all)

    def compose_step(running, pair):
        term, decay = pair
        updated = decay.astype(jnp.float32)[:, None, None] * running + term.astype(jnp.float32)
        return (updated, running)
    states_in = lax.scan(compose_step, zero_state, (all_ends, all_decays))[1]

    def middle_pass(pair):
        packed, state_in = pair
        normed, local_grad, grad_gated, pullback = segment_pass(packed, state_in, decay_rate, skip_weight, norm_gain)
        return (normed, local_grad)
    normed_all, local_grads = lax.map(middle_pass, (packed_all, states_in))
    states_grad = lax.scan(compose_step, zero_state, (local_grads, all_decays), reverse=True)[1]

    def final_pass(triple):
        packed, state_in, state_grad = triple
        normed, local_grad, grad_gated, pullback = segment_pass(packed, state_in, decay_rate, skip_weight, norm_gain)
        grads = pullback((grad_gated, state_grad))
        return tuple((item.astype(jnp.bfloat16) for item in grads))
    incoming_gradient, grad_gt, grad_keys, grad_queries = lax.map(final_pass, (packed_all, states_in, states_grad))
    return (normed_all.reshape(TOKENS, H * P_SIZE), incoming_gradient.reshape(TOKENS, H * P_SIZE), grad_gt.reshape(TOKENS, H * P_SIZE), grad_keys.reshape(TOKENS, G * N), grad_queries.reshape(TOKENS, G * N))
```

```python
import jax
import jax.numpy as jnp
from jax import lax
from jax.experimental import pallas as pl
from jax.experimental.pallas import tpu as pltpu
from jax.sharding import PartitionSpec as P

H = 256
P_SIZE = 64
N = 256
EPS = 1e-05
LOG2E = 1.4426950408889634

SEGS = 16
PARTS = 8
TOK = 512
HEADS = 32
COLS = HEADS * P_SIZE
SLICE = 128
TAIL = 16
WIDE = 256
STEPS = COLS // WIDE
HPS = WIDE // P_SIZE
SUB = 128
BLKS = TOK // SUB
HALF = TOK // 2

F32 = jnp.float32
BF16 = jnp.bfloat16
END, START, MIDDLE, QUARTER = range(4)


def nn(a, b):
    return jnp.dot(a, b, preferred_element_type=F32)


def nt(a, b):
    return lax.dot_general(a, b, (((1,), (1,)), ((), ())), preferred_element_type=F32)


def transposed(a):
    return a.astype(F32).T.astype(a.dtype)


def split(a):
    high = a.astype(BF16)
    return high, (a - high.astype(F32)).astype(BF16)


def expand(factors, which, step):
    row = lax.broadcasted_iota(jnp.int32, (2 * SLICE, WIDE), 0)
    head = (lax.broadcasted_iota(jnp.int32, (2 * SLICE, WIDE), 1) >> 6) + HPS * step
    pick = jnp.where((row & 127) == head + HEADS * which, 1.0, 0.0).astype(BF16)
    return nn(factors, pick)


def two_heads(a):
    lane = lax.broadcasted_iota(jnp.int32, a.shape, 1)
    zero = jnp.zeros_like(a)
    return jnp.concatenate([jnp.where(lane < P_SIZE, a, zero), jnp.where(lane < P_SIZE, zero, a)], 0)


def blk(i):
    return slice(i * SUB, (i + 1) * SUB)


def ends_kernel(step_ref, rate_ref, x_ref, keys_ref, out_ref, fac_ref, col_ref, row_ref, keys_t):
    step = pl.program_id(0)

    @pl.when(step == 0)
    def _():
        steps = step_ref[...]
        logs = steps * (rate_ref[...] * -LOG2E)
        high, rest = split(logs)
        rest = logs - high.astype(F32)
        mid, low = split(rest)
        source = lax.broadcasted_iota(jnp.int32, (TOK, TOK), 0)
        target = lax.broadcasted_iota(jnp.int32, (TOK, TOK), 1)
        upper = jnp.where(source <= target, 1.0, 0.0).astype(BF16)
        sums = nn(jnp.concatenate([high.astype(F32), mid.astype(F32), low.astype(F32)], 0).astype(BF16), upper)
        cum = sums[:HEADS] + sums[HEADS : 2 * HEADS] + sums[2 * HEADS :]
        shifted = cum - jnp.log(steps) * LOG2E
        token = lax.broadcasted_iota(jnp.int32, (HEADS, TOK), 1)
        one = jnp.ones_like(steps)
        end = jnp.exp2(cum[:, TOK - 1 :] - cum) * steps
        start = jnp.exp2(cum)
        middle = jnp.exp2(-jnp.abs(cum - cum[:, HALF - 1 : HALF])) * jnp.where(token < HALF, steps, one)
        near = jnp.where(token < HALF, cum[:, SUB - 1 : SUB], cum[:, 3 * SUB - 1 : 3 * SUB])
        quarter = jnp.exp2(-jnp.abs(cum - near)) * jnp.where((token & SUB) == 0, steps, one)
        high, low = split(jnp.concatenate([end, start, middle, quarter], 0).T)
        fac_ref[:, :128] = high
        fac_ref[:, 128:] = low
        col_ref[...] = jnp.concatenate([cum, shifted, cum, shifted], 0).T
        for part in range(STEPS):
            heads = slice(part * HPS, (part + 1) * HPS)
            row_ref[part] = jnp.concatenate([cum[heads], shifted[heads]], 0)
        keys_t[...] = transposed(keys_ref[...])

    factors = fac_ref[...]
    scaled = (x_ref[...].astype(F32) * expand(factors, END, step)).astype(BF16)
    ends = nn(keys_t[...], scaled).astype(BF16)
    decay = expand(factors[TOK - 16 :], START, step)
    decay = jnp.broadcast_to(decay[15:16], (TAIL, WIDE)).astype(BF16)
    for part in range(WIDE // SLICE):
        lanes = slice(part * SLICE, (part + 1) * SLICE)
        out_ref[part, :N] = ends[:, lanes]
        out_ref[part, N:] = decay[:, lanes]


def weights(col, row, scores):
    return (jnp.exp2(jnp.minimum(col - row, 0.0)) * scores).astype(BF16)


def local_kernel(x_ref, keys_ref, queries_ref, fac_ref, col_ref, row_ref, skip_ref, out_ref, near, off1, off2):
    step = pl.program_id(0)

    @pl.when(step == 0)
    def _():
        target = lax.broadcasted_iota(jnp.int32, (SUB, SUB), 0)
        source = lax.broadcasted_iota(jnp.int32, (SUB, SUB), 1)
        for i in range(BLKS):
            scores = nt(queries_ref[blk(i)], keys_ref[blk(i)])
            near[i] = jnp.where(source <= target, scores, 0.0)
        for i in range(BLKS // 2):
            off1[i] = nt(queries_ref[blk(2 * i + 1)], keys_ref[blk(2 * i)]).astype(BF16)
        off2[...] = nt(queries_ref[HALF:], keys_ref[:HALF]).astype(BF16)

    factors = fac_ref[...]
    x = x_ref[...]
    wide = x.astype(F32)
    middle = expand(factors, MIDDLE, step)
    quarter = expand(factors, QUARTER, step)
    cols = pltpu.roll(col_ref[...], lax.rem(128 - HPS * step, 128), 1)
    far = nn(off2[...], (wide[:HALF] * middle[:HALF]).astype(BF16)) * middle[HALF:]
    skip = skip_ref[...] * wide
    for i in range(BLKS):
        total = skip[blk(i)]
        if i % 2:
            before = (wide[blk(i - 1)] * quarter[blk(i - 1)]).astype(BF16)
            total += nn(off1[i // 2], before) * quarter[blk(i)]
        if i >= 2:
            total += far[blk(i - 2)]
        scores = near[i]
        for pair in range(WIDE // SLICE):
            lanes = slice(pair * SLICE, (pair + 1) * SLICE)
            both = []
            for j in (2 * pair, 2 * pair + 1):
                row = row_ref[0, HPS + j : HPS + j + 1, blk(i)]
                both.append(weights(cols[blk(i), j : j + 1], row, scores))
            within = nn(jnp.concatenate(both, 1), two_heads(x[blk(i), lanes]))
            out_ref[blk(i), lanes] = total[:, lanes] + within


def forward_scan_kernel(in_ref, out_ref):
    running = jnp.zeros((N, SLICE), F32)
    for k in range(SEGS):
        out_ref[k] = running.astype(BF16)
        decay = in_ref[k, N : N + TAIL][:1].astype(F32)
        running = running * decay + in_ref[k, :N].astype(F32)


def backward_scan_kernel(in_ref, decay_ref, out_ref):
    running = jnp.zeros((N, SLICE), F32)
    for k in reversed(range(SEGS)):
        out_ref[k] = running.astype(BF16)
        running = running * decay_ref[k][:1].astype(F32) + in_ref[k].astype(F32)


def state_of(ref):
    return jnp.concatenate([ref[part] for part in range(WIDE // SLICE)], 1)


def gate_kernel(local_ref, state_ref, queries_ref, fac_ref, gate_ref, gain_ref, grad_ref, mixed_ref, sums_ref, square, product):
    step = pl.program_id(0)

    @pl.when(step == 0)
    def _():
        square[...] = jnp.zeros_like(square)
        product[...] = jnp.zeros_like(product)

    carried = nn(queries_ref[...], state_of(state_ref)) * expand(fac_ref[...], START, step)
    mixed = local_ref[...] + carried
    mixed_ref[...] = mixed
    gate = gate_ref[...].astype(F32)
    gated = mixed * (gate * jax.nn.sigmoid(gate))
    squares = gated * gated
    products = gated * (gain_ref[...] * grad_ref[...].astype(F32))
    square[...] += squares[:, :128] + squares[:, 128:]
    product[...] += products[:, :128] + products[:, 128:]

    @pl.when(step == STEPS - 1)
    def _():
        both = jnp.concatenate(
            [jnp.sum(square[...].T, axis=0, keepdims=True), jnp.sum(product[...].T, axis=0, keepdims=True)], 0
        )
        for part in range(PARTS):
            sums_ref[part] = both


def norm_terms(sums_ref, inverse, slope):
    total = sums_ref[0]
    for part in range(1, PARTS):
        total += sums_ref[part]
    inv_rms = lax.rsqrt(total[:1] / (H * P_SIZE) + EPS)
    ratio = inv_rms * inv_rms * inv_rms * total[1:] / (H * P_SIZE)
    inverse[...] = jnp.broadcast_to(inv_rms, (128, TOK)).T
    slope[...] = jnp.broadcast_to(ratio, (128, TOK)).T


def wide_of(ref):
    return jnp.concatenate([ref[...]] * (WIDE // 128), 1)


def grad_kernel(mixed_ref, sums_ref, queries_ref, fac_ref, gate_ref, gain_ref, grad_ref, dy_ref, out_ref, inverse, slope, queries_t):
    step = pl.program_id(0)

    @pl.when(step == 0)
    def _():
        norm_terms(sums_ref, inverse, slope)
        queries_t[...] = transposed(queries_ref[...])

    gate = gate_ref[...].astype(F32)
    silu = gate * jax.nn.sigmoid(gate)
    gated = mixed_ref[...] * silu
    grad_gated = wide_of(inverse) * (gain_ref[...] * grad_ref[...].astype(F32)) - gated * wide_of(slope)
    dy = grad_gated * silu
    dy_ref[...] = dy.astype(BF16)
    weighted = (dy * expand(fac_ref[...], START, step)).astype(BF16)
    local = nn(queries_t[...], weighted).astype(BF16)
    for part in range(WIDE // SLICE):
        out_ref[part] = local[:, part * SLICE : (part + 1) * SLICE]


def norm_kernel(mixed_ref, sums_ref, gate_ref, gain_ref, grad_ref, normed_ref, out_ref, inverse, slope):
    step = pl.program_id(0)

    @pl.when(step == 0)
    def _():
        norm_terms(sums_ref, inverse, slope)

    gate = gate_ref[...].astype(F32)
    sig = jax.nn.sigmoid(gate)
    mixed = mixed_ref[...]
    gated = mixed * (gate * sig)
    gain = wide_of(inverse) * gain_ref[...]
    normed_ref[...] = (gated * gain).astype(BF16)
    grad_gated = gain * grad_ref[...].astype(F32) - gated * wide_of(slope)
    out_ref[...] = (grad_gated * mixed * (sig * (1.0 + gate * (1.0 - sig)))).astype(BF16)


def back_kernel(
    x_ref, dy_ref, state_ref, keys_ref, queries_ref, fac_ref, col_ref, row_ref, skip_ref,
    dx_ref, scaled_ref, dkeys_ref, dqueries_ref,
    near, off1, off2, dnear, doff1, doff2, dq,
):
    step = pl.program_id(0)

    @pl.when(step == 0)
    def _():
        source = lax.broadcasted_iota(jnp.int32, (SUB, SUB), 0)
        target = lax.broadcasted_iota(jnp.int32, (SUB, SUB), 1)
        for i in range(BLKS):
            scores = nt(keys_ref[blk(i)], queries_ref[blk(i)])
            near[i] = jnp.where(source <= target, scores, 0.0)
        for i in range(BLKS // 2):
            off1[i] = nt(keys_ref[blk(2 * i)], queries_ref[blk(2 * i + 1)]).astype(BF16)
        off2[...] = nt(keys_ref[:HALF], queries_ref[HALF:]).astype(BF16)
        dnear[...] = jnp.zeros_like(dnear)
        doff1[...] = jnp.zeros_like(doff1)
        doff2[...] = jnp.zeros_like(doff2)
        dq[...] = jnp.zeros_like(dq)

    factors = fac_ref[...]
    x = x_ref[...]
    wide = x.astype(F32)
    dy = dy_ref[...]
    dwide = dy.astype(F32)
    scaled_ref[...] = (wide * expand(factors, END, step)).astype(BF16)
    weighted = (dwide * expand(factors, START, step)).astype(BF16)
    dq[...] += nt(weighted, state_of(state_ref))
    middle = expand(factors, MIDDLE, step)
    quarter = expand(factors, QUARTER, step)
    cols = pltpu.roll(col_ref[...], lax.rem(128 - HPS * step, 128), 1)
    above = (wide[:HALF] * middle[:HALF]).astype(BF16)
    below = (dwide[HALF:] * middle[HALF:]).astype(BF16)
    far = nn(off2[...], below) * middle[:HALF]
    doff2[...] += nt(above, below)
    skip = skip_ref[...] * dwide
    for i in range(BLKS):
        total = skip[blk(i)]
        if i % 2 == 0:
            above = (wide[blk(i)] * quarter[blk(i)]).astype(BF16)
            below = (dwide[blk(i + 1)] * quarter[blk(i + 1)]).astype(BF16)
            total += nn(off1[i // 2], below) * quarter[blk(i)]
            doff1[i // 2] += nt(above, below)
        if i < 2:
            total += far[blk(i)]
        scores = near[i]
        dscores = dnear[i]
        for pair in range(WIDE // SLICE):
            lanes = slice(pair * SLICE, (pair + 1) * SLICE)
            dy_two = two_heads(dy[blk(i), lanes])
            dweights = nt(x[blk(i), lanes], dy_two)
            both = []
            for place, j in enumerate((2 * pair, 2 * pair + 1)):
                row = row_ref[0, j : j + 1, blk(i)]
                decay = jnp.exp2(jnp.minimum(row - cols[blk(i), HEADS + j : HEADS + j + 1], 0.0))
                both.append((decay * scores).astype(BF16))
                dscores += decay * dweights[:, place * SUB : (place + 1) * SUB]
            dx_ref[blk(i), lanes] = total[:, lanes] + nn(jnp.concatenate(both, 1), dy_two)
        dnear[i] = dscores

    @pl.when(step == STEPS - 1)
    def _():
        source = lax.broadcasted_iota(jnp.int32, (SUB, SUB), 0)
        target = lax.broadcasted_iota(jnp.int32, (SUB, SUB), 1)
        last = doff2[...]
        dkeys_ref[...] = jnp.zeros_like(dkeys_ref)
        dkeys_ref[:HALF] += nn(last.astype(BF16), queries_ref[HALF:])
        dq[HALF:] += nn(last.T.astype(BF16), keys_ref[:HALF])
        for i in range(BLKS // 2):
            part = doff1[i]
            dkeys_ref[blk(2 * i)] += nn(part.astype(BF16), queries_ref[blk(2 * i + 1)])
            dq[blk(2 * i + 1)] += nn(part.T.astype(BF16), keys_ref[blk(2 * i)])
        for i in range(BLKS):
            part = jnp.where(source <= target, dnear[i], 0.0)
            dkeys_ref[blk(i)] += nn(part.astype(BF16), queries_ref[blk(i)])
            dq[blk(i)] += nn(part.T.astype(BF16), keys_ref[blk(i)])
        dqueries_ref[...] = dq[...].astype(BF16)


def final_kernel(dx_ref, scaled_ref, grad_ref, keys_ref, fac_ref, dkeys_ref, out_ref, out_keys_ref, total):
    step = pl.program_id(0)

    @pl.when(step == 0)
    def _():
        total[...] = dkeys_ref[...]

    state_grad = state_of(grad_ref)
    from_end = nn(keys_ref[...], state_grad) * expand(fac_ref[...], END, step)
    out_ref[...] = (dx_ref[...] + from_end).astype(BF16)
    total[...] += nt(scaled_ref[...], state_grad)

    @pl.when(step == STEPS - 1)
    def _():
        out_keys_ref[...] = total[...].astype(BF16)


def whole(shape):
    return pl.BlockSpec(shape, lambda i: (0,) * len(shape))


TOKENS_BY_STEP = pl.BlockSpec((TOK, WIDE), lambda i: (0, i))
ROW_BY_STEP = pl.BlockSpec((1, WIDE), lambda i: (0, i))
MAP = whole((TOK, N))
FACTORS = whole((TOK, 2 * SLICE))
COLUMNS = whole((TOK, 128))
ROWS = whole((STEPS, 2 * HPS, TOK))
ROWS_BY_STEP = pl.BlockSpec((1, 2 * HPS, TOK), lambda i: (i, 0, 0))
SUMS = whole((PARTS, 2, TOK))


def state_by_step(rows):
    return pl.BlockSpec((WIDE // SLICE, rows, SLICE), lambda i: (i, 0, 0))


def shape(*dims, dtype=F32):
    return jax.ShapeDtypeStruct(dims, dtype)


def call(kernel, name, in_specs, out_specs, out_shape, scratch=(), gmacs=1.0, mib=8.0, limit=24):
    return pl.pallas_call(
        kernel,
        name=name,
        grid=(STEPS,),
        in_specs=in_specs,
        out_specs=out_specs,
        out_shape=out_shape,
        scratch_shapes=list(scratch),
        compiler_params=pltpu.CompilerParams(vmem_limit_bytes=limit << 20),
        cost_estimate=pl.CostEstimate(flops=int(2e9 * gmacs), bytes_accessed=int(mib * 2**20), transcendentals=0),
    )


def whole_call(kernel, name, in_specs, out_specs, out_shape):
    return pl.pallas_call(
        kernel,
        name=name,
        grid=(1,),
        in_specs=in_specs,
        out_specs=out_specs,
        out_shape=out_shape,
        compiler_params=pltpu.CompilerParams(vmem_limit_bytes=16 << 20),
        cost_estimate=pl.CostEstimate(flops=2**24, bytes_accessed=2**21, transcendentals=0),
    )


def exchange(a, axis):
    return lax.all_to_all(a, axis, 0, 0)


def body(inputs, gate_input, step_size, input_map, output_map, decay_rate, skip_weight, norm_gain, out_grad):
    rate = decay_rate.reshape(HEADS, 1)
    gain = norm_gain.reshape(1, COLS)
    skip = jnp.repeat(skip_weight, P_SIZE).reshape(1, COLS)
    tokens = shape(TOK, COLS)
    tokens_out = shape(TOK, COLS, dtype=BF16)
    score_scratch = [
        pltpu.VMEM((BLKS, SUB, SUB), F32),
        pltpu.VMEM((BLKS // 2, SUB, SUB), BF16),
        pltpu.VMEM((HALF, HALF), BF16),
    ]
    norm_scratch = [pltpu.VMEM((TOK, 128), F32)] * 2

    ends, factors, columns, rows = call(
        ends_kernel,
        "segment_ends",
        [whole((HEADS, TOK)), whole((HEADS, 1)), TOKENS_BY_STEP, MAP],
        [state_by_step(N + TAIL), FACTORS, COLUMNS, ROWS],
        [shape(SEGS, N + TAIL, SLICE, dtype=BF16), shape(TOK, 2 * SLICE, dtype=BF16), shape(TOK, 128), shape(STEPS, 2 * HPS, TOK)],
        [pltpu.VMEM((N, TOK), BF16)],
    )(step_size, rate, inputs, input_map)
    all_ends = exchange(ends, "ctx")

    mixed_local = call(
        local_kernel,
        "within_segment",
        [TOKENS_BY_STEP, MAP, MAP, FACTORS, COLUMNS, ROWS_BY_STEP, ROW_BY_STEP],
        TOKENS_BY_STEP,
        tokens,
        score_scratch,
        gmacs=4.0,
    )(inputs, input_map, output_map, factors, columns, rows, skip)

    starts = whole_call(
        forward_scan_kernel,
        "forward_scan",
        [whole((SEGS, N + TAIL, SLICE))],
        whole((SEGS, N, SLICE)),
        shape(SEGS, N, SLICE, dtype=BF16),
    )(all_ends)
    state_in = exchange(starts, "ctx")

    mixed, sums = call(
        gate_kernel,
        "carry_and_gate",
        [TOKENS_BY_STEP, state_by_step(N), MAP, FACTORS, TOKENS_BY_STEP, ROW_BY_STEP, TOKENS_BY_STEP],
        [TOKENS_BY_STEP, SUMS],
        [tokens, shape(PARTS, 2, TOK)],
        norm_scratch,
    )(mixed_local, state_in, output_map, factors, gate_input, gain, out_grad)
    sums = exchange(sums, "tp")

    dy, local_grads = call(
        grad_kernel,
        "local_grads",
        [TOKENS_BY_STEP, SUMS, MAP, FACTORS, TOKENS_BY_STEP, ROW_BY_STEP, TOKENS_BY_STEP],
        [TOKENS_BY_STEP, state_by_step(N)],
        [tokens_out, shape(SEGS, N, SLICE, dtype=BF16)],
        norm_scratch + [pltpu.VMEM((N, TOK), BF16)],
    )(mixed, sums, output_map, factors, gate_input, gain, out_grad)
    all_grads = exchange(local_grads, "ctx")

    normed, grad_gate = call(
        norm_kernel,
        "normed_and_gate",
        [TOKENS_BY_STEP, SUMS, TOKENS_BY_STEP, ROW_BY_STEP, TOKENS_BY_STEP],
        [TOKENS_BY_STEP, TOKENS_BY_STEP],
        [tokens_out, tokens_out],
        norm_scratch,
    )(mixed, sums, gate_input, gain, out_grad)

    dx, scaled, dkeys, dqueries = call(
        back_kernel,
        "within_segment_back",
        [TOKENS_BY_STEP, TOKENS_BY_STEP, state_by_step(N), MAP, MAP, FACTORS, COLUMNS, ROWS_BY_STEP, ROW_BY_STEP],
        [TOKENS_BY_STEP, TOKENS_BY_STEP, MAP, MAP],
        [tokens, tokens_out, shape(TOK, N), shape(TOK, N, dtype=BF16)],
        score_scratch
        + [
            pltpu.VMEM((BLKS, SUB, SUB), F32),
            pltpu.VMEM((BLKS // 2, SUB, SUB), F32),
            pltpu.VMEM((HALF, HALF), F32),
            pltpu.VMEM((TOK, N), F32),
        ],
        gmacs=6.0,
    )(inputs, dy, state_in, input_map, output_map, factors, columns, rows, skip)

    grad_starts = whole_call(
        backward_scan_kernel,
        "backward_scan",
        [whole((SEGS, N, SLICE)), pl.BlockSpec((SEGS, TAIL, SLICE), lambda i: (0, N // TAIL, 0))],
        whole((SEGS, N, SLICE)),
        shape(SEGS, N, SLICE, dtype=BF16),
    )(all_grads, all_ends)
    state_grad = exchange(grad_starts, "ctx")

    grad_inputs, grad_keys = call(
        final_kernel,
        "final_grads",
        [TOKENS_BY_STEP, TOKENS_BY_STEP, state_by_step(N), MAP, FACTORS, MAP],
        [TOKENS_BY_STEP, MAP],
        [tokens_out, shape(TOK, N, dtype=BF16)],
        [pltpu.VMEM((TOK, N), F32)],
    )(dx, scaled, state_grad, input_map, factors, dkeys)
    return normed, grad_inputs, grad_gate, grad_keys, dqueries


def solution(mesh):
    both = P("ctx", "tp")
    return jax.shard_map(
        body,
        mesh=mesh,
        in_specs=(both, both, P("tp", "ctx"), both, both, P("tp"), P("tp"), P("tp"), both),
        out_specs=(both,) * 5,
        check_vma=False,
    )
```

```python
import jax
import jax.numpy as jnp
from jax import lax
from jax.experimental import pallas as pl
from jax.experimental.pallas import tpu as pltpu
from jax.sharding import PartitionSpec as P

H = 256
P_SIZE = 64
N = 256
EPS = 1e-05
LOG2E = 1.4426950408889634

SEGS = 16
PARTS = 8
TOK = 512
HEADS = 32
COLS = HEADS * P_SIZE
SLICE = 128
TAIL = 16
WIDE = 256
LONG = 1024
STEPS = COLS // WIDE
CHUNKS = COLS // LONG
HPS = WIDE // P_SIZE
VMEM_MIB = 36
SUB = 128
BLKS = TOK // SUB
HALF = TOK // 2

F32 = jnp.float32
BF16 = jnp.bfloat16
END, START, MIDDLE, QUARTER = range(4)


def nn(a, b):
    return jnp.dot(a, b, preferred_element_type=F32)


def nt(a, b):
    return lax.dot_general(a, b, (((1,), (1,)), ((), ())), preferred_element_type=F32)


def transposed(a):
    return a.astype(F32).T.astype(a.dtype)


def split(a):
    high = a.astype(BF16)
    return high, (a - high.astype(F32)).astype(BF16)


def expand(factors, which, step, width):
    row = lax.broadcasted_iota(jnp.int32, (2 * SLICE, width), 0)
    head = (lax.broadcasted_iota(jnp.int32, (2 * SLICE, width), 1) >> 6) + (width // P_SIZE) * step
    pick = jnp.where((row & 127) == head + HEADS * which, 1.0, 0.0).astype(BF16)
    return nn(factors, pick)


def two_heads(a):
    lane = lax.broadcasted_iota(jnp.int32, a.shape, 1)
    zero = jnp.zeros_like(a)
    return jnp.concatenate([jnp.where(lane < P_SIZE, a, zero), jnp.where(lane < P_SIZE, zero, a)], 0)


def blk(i):
    return slice(i * SUB, (i + 1) * SUB)


def columns_of(array, chunk):
    return array.at[:, pl.ds(pl.multiple_of(chunk * LONG, LONG), LONG)]


def slices_of(array, chunk):
    return array.at[pl.ds(chunk * (LONG // SLICE), LONG // SLICE)]


def ends_kernel(
    step_in, rate_in, x_in, keys_in, out, fac_out, col_out, row_out,
    step_ref, rate_ref, x_ref, keys_ref, ends_ref, fac_ref, col_ref, row_ref, keys_t, small, come, go,
):
    def fetch(chunk):
        return pltpu.make_async_copy(columns_of(x_in, chunk), x_ref.at[chunk], come.at[chunk])

    def send(chunk):
        return pltpu.make_async_copy(slices_of(ends_ref, chunk), slices_of(out, chunk), go.at[chunk])

    pairs = [(step_in, step_ref), (rate_in, rate_ref), (keys_in, keys_ref)]
    pairs += [(fac_ref, fac_out), (col_ref, col_out), (row_ref, row_out)]
    copies = [pltpu.make_async_copy(a, b, small.at[i]) for i, (a, b) in enumerate(pairs)]
    for copy in copies[:3]:
        copy.start()
    for chunk in range(CHUNKS):
        fetch(chunk).start()
    copies[0].wait()
    copies[1].wait()

    steps = step_ref[...]
    diagonal = lax.broadcasted_iota(jnp.int32, (HEADS, HEADS), 0) == lax.broadcasted_iota(jnp.int32, (HEADS, HEADS), 1)
    rate = jnp.sum(jnp.where(diagonal, rate_ref[...], 0.0), axis=1, keepdims=True)
    logs = steps * (rate * -LOG2E)
    high = logs.astype(BF16)
    rest = logs - high.astype(F32)
    mid, low = split(rest)
    source = lax.broadcasted_iota(jnp.int32, (TOK, TOK), 0)
    target = lax.broadcasted_iota(jnp.int32, (TOK, TOK), 1)
    upper = jnp.where(source <= target, 1.0, 0.0).astype(BF16)
    sums = nn(jnp.concatenate([high.astype(F32), mid.astype(F32), low.astype(F32)], 0).astype(BF16), upper)
    cum = sums[:HEADS] + sums[HEADS : 2 * HEADS] + sums[2 * HEADS :]
    shifted = cum - jnp.log(steps) * LOG2E
    token = lax.broadcasted_iota(jnp.int32, (HEADS, TOK), 1)
    one = jnp.ones_like(steps)
    end = jnp.exp2(cum[:, TOK - 1 :] - cum) * steps
    start = jnp.exp2(cum)
    middle = jnp.exp2(-jnp.abs(cum - cum[:, HALF - 1 : HALF])) * jnp.where(token < HALF, steps, one)
    near = jnp.where(token < HALF, cum[:, SUB - 1 : SUB], cum[:, 3 * SUB - 1 : 3 * SUB])
    quarter = jnp.exp2(-jnp.abs(cum - near)) * jnp.where((token & SUB) == 0, steps, one)
    high, low = split(jnp.concatenate([end, start, middle, quarter], 0).T)
    fac_ref[:, :128] = high
    fac_ref[:, 128:] = low
    copies[3].start()
    copies[2].wait()
    keys_t[...] = transposed(keys_ref[...])

    @pl.loop(0, CHUNKS)
    def _(chunk):
        fetch(chunk).wait()
        factors = fac_ref[...]
        scaled = (x_ref[chunk].astype(F32) * expand(factors, END, chunk, LONG)).astype(BF16)
        ends = nn(keys_t[...], scaled).astype(BF16)
        decay = expand(factors[TOK - 16 :], START, chunk, LONG)
        decay = jnp.broadcast_to(decay[15:16], (TAIL, LONG)).astype(BF16)
        for part in range(LONG // SLICE):
            lanes = slice(part * SLICE, (part + 1) * SLICE)
            ends_ref[chunk * (LONG // SLICE) + part, :N] = ends[:, lanes]
            ends_ref[chunk * (LONG // SLICE) + part, N:] = decay[:, lanes]
        send(chunk).start()

    col_ref[...] = jnp.concatenate([cum, shifted, cum, shifted], 0).T
    for part in range(STEPS):
        heads = slice(part * HPS, (part + 1) * HPS)
        row_ref[part] = jnp.concatenate([cum[heads], shifted[heads]], 0)
    copies[4].start()
    copies[5].start()
    for copy in copies[3:]:
        copy.wait()
    for chunk in range(CHUNKS):
        send(chunk).wait()


def weights(col, row, scores):
    return (jnp.exp2(jnp.minimum(col - row, 0.0)) * scores).astype(BF16)


def local_kernel(x_ref, gate_ref, keys_ref, queries_ref, fac_ref, col_ref, row_ref, skip_ref, out_ref, silu_ref, scaled_ref, near, off1, off2):
    step = pl.program_id(0)

    @pl.when(step == 0)
    def _():
        target = lax.broadcasted_iota(jnp.int32, (SUB, SUB), 0)
        source = lax.broadcasted_iota(jnp.int32, (SUB, SUB), 1)
        for i in range(BLKS):
            scores = nt(queries_ref[blk(i)], keys_ref[blk(i)])
            near[i] = jnp.where(source <= target, scores, 0.0)
        for i in range(BLKS // 2):
            off1[i] = nt(queries_ref[blk(2 * i + 1)], keys_ref[blk(2 * i)]).astype(BF16)
        off2[...] = nt(queries_ref[HALF:], keys_ref[:HALF]).astype(BF16)

    factors = fac_ref[...]
    x = x_ref[...]
    wide = x.astype(F32)
    middle = expand(factors, MIDDLE, step, WIDE)
    quarter = expand(factors, QUARTER, step, WIDE)
    cols = pltpu.roll(col_ref[...], lax.rem(128 - HPS * step, 128), 1)
    scaled_ref[...] = (wide * expand(factors, END, step, WIDE)).astype(BF16)
    gate = gate_ref[...].astype(F32)
    silu_ref[...] = (gate * jax.nn.sigmoid(gate)).astype(BF16)
    far = nn(off2[...], (wide[:HALF] * middle[:HALF]).astype(BF16)) * middle[HALF:]
    skip = skip_ref[...] * wide
    for i in range(BLKS):
        total = skip[blk(i)]
        if i % 2:
            before = (wide[blk(i - 1)] * quarter[blk(i - 1)]).astype(BF16)
            total += nn(off1[i // 2], before) * quarter[blk(i)]
        if i >= 2:
            total += far[blk(i - 2)]
        scores = near[i]
        for pair in range(WIDE // SLICE):
            lanes = slice(pair * SLICE, (pair + 1) * SLICE)
            both = []
            for j in (2 * pair, 2 * pair + 1):
                row = row_ref[0, HPS + j : HPS + j + 1, blk(i)]
                both.append(weights(cols[blk(i), j : j + 1], row, scores))
            within = nn(jnp.concatenate(both, 1), two_heads(x[blk(i), lanes]))
            out_ref[blk(i), lanes] = (total[:, lanes] + within).astype(BF16)


def forward_scan_kernel(in_ref, out_ref):
    running = jnp.zeros((N, SLICE), F32)
    for k in range(SEGS):
        out_ref[k] = running.astype(BF16)
        decay = in_ref[k, N : N + TAIL][:1].astype(F32)
        running = running * decay + in_ref[k, :N].astype(F32)


def backward_scan_kernel(in_ref, decay_ref, out_ref):
    running = jnp.zeros((N, SLICE), F32)
    for k in reversed(range(SEGS)):
        out_ref[k] = running.astype(BF16)
        running = running * decay_ref[k][:1].astype(F32) + in_ref[k].astype(F32)


def state_of(ref):
    return jnp.concatenate([ref[part] for part in range(ref.shape[0])], 1)


def fold(a):
    total = a[:, :128]
    for lane in range(128, a.shape[1], 128):
        total += a[:, lane : lane + 128]
    return total


def gate_kernel(local_ref, state_ref, queries_ref, fac_ref, silu_ref, gain_ref, grad_ref, mixed_ref, sums_ref, square, product):
    step = pl.program_id(0)

    @pl.when(step == 0)
    def _():
        square[...] = jnp.zeros_like(square)
        product[...] = jnp.zeros_like(product)

    carried = nn(queries_ref[...], state_of(state_ref)) * expand(fac_ref[...], START, step, LONG)
    mixed = local_ref[...].astype(F32) + carried
    mixed_ref[...] = mixed.astype(BF16)
    gated = mixed * silu_ref[...].astype(F32)
    squares = gated * gated
    products = gated * (gain_ref[...] * grad_ref[...].astype(F32))
    square[...] += fold(squares)
    product[...] += fold(products)

    @pl.when(step == COLS // LONG - 1)
    def _():
        both = jnp.concatenate(
            [jnp.sum(square[...].T, axis=0, keepdims=True), jnp.sum(product[...].T, axis=0, keepdims=True)], 0
        )
        for part in range(PARTS):
            sums_ref[part] = both


def norm_terms(sums_ref, inverse, slope):
    total = sums_ref[0]
    for part in range(1, PARTS):
        total += sums_ref[part]
    inv_rms = lax.rsqrt(total[:1] / (H * P_SIZE) + EPS)
    ratio = inv_rms * inv_rms * inv_rms * total[1:] / (H * P_SIZE)
    inverse[...] = jnp.broadcast_to(inv_rms, (128, TOK)).T
    slope[...] = jnp.broadcast_to(ratio, (128, TOK)).T


def wide_of(ref):
    return jnp.concatenate([ref[...]] * (LONG // 128), 1)


def grad_kernel(mixed_ref, sums_ref, queries_ref, fac_ref, silu_ref, gain_ref, grad_ref, dy_ref, out_ref, inverse, slope, queries_t):
    step = pl.program_id(0)

    @pl.when(step == 0)
    def _():
        norm_terms(sums_ref, inverse, slope)
        queries_t[...] = transposed(queries_ref[...])

    silu = silu_ref[...].astype(F32)
    gated = mixed_ref[...].astype(F32) * silu
    grad_gated = wide_of(inverse) * (gain_ref[...] * grad_ref[...].astype(F32)) - gated * wide_of(slope)
    dy = grad_gated * silu
    dy_ref[...] = dy.astype(BF16)
    weighted = (dy * expand(fac_ref[...], START, step, LONG)).astype(BF16)
    local = nn(queries_t[...], weighted).astype(BF16)
    for part in range(LONG // SLICE):
        out_ref[part] = local[:, part * SLICE : (part + 1) * SLICE]


def norm_kernel(mixed_ref, sums_ref, gate_ref, gain_ref, grad_ref, normed_ref, out_ref, inverse, slope):
    step = pl.program_id(0)

    @pl.when(step == 0)
    def _():
        norm_terms(sums_ref, inverse, slope)

    gate = gate_ref[...].astype(F32)
    sig = jax.nn.sigmoid(gate)
    mixed = mixed_ref[...].astype(F32)
    gated = mixed * (gate * sig)
    gain = wide_of(inverse) * gain_ref[...]
    normed_ref[...] = (gated * gain).astype(BF16)
    grad_gated = gain * grad_ref[...].astype(F32) - gated * wide_of(slope)
    out_ref[...] = (grad_gated * mixed * (sig * (1.0 + gate * (1.0 - sig)))).astype(BF16)


def back_kernel(
    x_ref, dy_ref, state_ref, keys_ref, queries_ref, fac_ref, col_ref, row_ref, skip_ref,
    dx_ref, dkeys_ref, dqueries_ref,
    near, off1, off2, dnear, doff1, doff2, dq,
):
    step = pl.program_id(0)

    @pl.when(step == 0)
    def _():
        source = lax.broadcasted_iota(jnp.int32, (SUB, SUB), 0)
        target = lax.broadcasted_iota(jnp.int32, (SUB, SUB), 1)
        for i in range(BLKS):
            scores = nt(keys_ref[blk(i)], queries_ref[blk(i)])
            near[i] = jnp.where(source <= target, scores, 0.0)
        for i in range(BLKS // 2):
            off1[i] = nt(keys_ref[blk(2 * i)], queries_ref[blk(2 * i + 1)]).astype(BF16)
        off2[...] = nt(keys_ref[:HALF], queries_ref[HALF:]).astype(BF16)
        dnear[...] = jnp.zeros_like(dnear)
        doff1[...] = jnp.zeros_like(doff1)
        doff2[...] = jnp.zeros_like(doff2)
        dq[...] = jnp.zeros_like(dq)

    factors = fac_ref[...]
    x = x_ref[...]
    wide = x.astype(F32)
    dy = dy_ref[...]
    dwide = dy.astype(F32)
    weighted = (dwide * expand(factors, START, step, WIDE)).astype(BF16)
    dq[...] += nt(weighted, state_of(state_ref))
    middle = expand(factors, MIDDLE, step, WIDE)
    quarter = expand(factors, QUARTER, step, WIDE)
    cols = pltpu.roll(col_ref[...], lax.rem(128 - HPS * step, 128), 1)
    above = (wide[:HALF] * middle[:HALF]).astype(BF16)
    below = (dwide[HALF:] * middle[HALF:]).astype(BF16)
    far = nn(off2[...], below) * middle[:HALF]
    doff2[...] += nt(above, below)
    skip = skip_ref[...] * dwide
    for i in range(BLKS):
        total = skip[blk(i)]
        if i % 2 == 0:
            above = (wide[blk(i)] * quarter[blk(i)]).astype(BF16)
            below = (dwide[blk(i + 1)] * quarter[blk(i + 1)]).astype(BF16)
            total += nn(off1[i // 2], below) * quarter[blk(i)]
            doff1[i // 2] += nt(above, below)
        if i < 2:
            total += far[blk(i)]
        scores = near[i]
        dscores = dnear[i]
        for pair in range(WIDE // SLICE):
            lanes = slice(pair * SLICE, (pair + 1) * SLICE)
            dy_two = two_heads(dy[blk(i), lanes])
            dweights = nt(x[blk(i), lanes], dy_two)
            both = []
            for place, j in enumerate((2 * pair, 2 * pair + 1)):
                row = row_ref[0, j : j + 1, blk(i)]
                decay = jnp.exp2(jnp.minimum(row - cols[blk(i), HEADS + j : HEADS + j + 1], 0.0))
                both.append((decay * scores).astype(BF16))
                dscores += decay * dweights[:, place * SUB : (place + 1) * SUB]
            dx_ref[blk(i), lanes] = (total[:, lanes] + nn(jnp.concatenate(both, 1), dy_two)).astype(BF16)
        dnear[i] = dscores

    @pl.when(step == STEPS - 1)
    def _():
        source = lax.broadcasted_iota(jnp.int32, (SUB, SUB), 0)
        target = lax.broadcasted_iota(jnp.int32, (SUB, SUB), 1)
        last = doff2[...]
        dkeys_ref[...] = jnp.zeros_like(dkeys_ref)
        dkeys_ref[:HALF] += nn(last.astype(BF16), queries_ref[HALF:])
        dq[HALF:] += nn(last.T.astype(BF16), keys_ref[:HALF])
        for i in range(BLKS // 2):
            part = doff1[i]
            dkeys_ref[blk(2 * i)] += nn(part.astype(BF16), queries_ref[blk(2 * i + 1)])
            dq[blk(2 * i + 1)] += nn(part.T.astype(BF16), keys_ref[blk(2 * i)])
        for i in range(BLKS):
            part = jnp.where(source <= target, dnear[i], 0.0)
            dkeys_ref[blk(i)] += nn(part.astype(BF16), queries_ref[blk(i)])
            dq[blk(i)] += nn(part.T.astype(BF16), keys_ref[blk(i)])
        dqueries_ref[...] = dq[...].astype(BF16)


def final_kernel(
    dx_in, scaled_in, grad_in, keys_in, fac_in, dkeys_in, out, out_keys,
    dx_ref, scaled_ref, grad_ref, keys_ref, fac_ref, dkeys_ref, out_ref, out_keys_ref, total, small, come, go,
):
    def fetch(chunk):
        return (
            pltpu.make_async_copy(slices_of(grad_in, chunk), slices_of(grad_ref, chunk), come.at[0, chunk]),
            pltpu.make_async_copy(columns_of(scaled_in, chunk), scaled_ref.at[chunk], come.at[1, chunk]),
            pltpu.make_async_copy(columns_of(dx_in, chunk), dx_ref.at[chunk], come.at[2, chunk]),
        )

    def send(chunk):
        return pltpu.make_async_copy(out_ref.at[chunk], columns_of(out, chunk), go.at[chunk])

    pairs = [(keys_in, keys_ref), (fac_in, fac_ref), (dkeys_in, dkeys_ref), (out_keys_ref, out_keys)]
    copies = [pltpu.make_async_copy(a, b, small.at[i]) for i, (a, b) in enumerate(pairs)]
    copies[0].start()
    copies[1].start()
    for chunk in range(CHUNKS):
        for copy in fetch(chunk):
            copy.start()
    copies[2].start()
    total[...] = jnp.zeros_like(total)
    copies[0].wait()
    copies[1].wait()

    @pl.loop(0, CHUNKS)
    def _(chunk):
        for copy in fetch(chunk):
            copy.wait()
        first = chunk * (LONG // SLICE)
        state_grad = jnp.concatenate([grad_ref[first + part] for part in range(LONG // SLICE)], 1)
        from_end = nn(keys_ref[...], state_grad) * expand(fac_ref[...], END, chunk, LONG)
        out_ref[chunk] = (dx_ref[chunk].astype(F32) + from_end).astype(BF16)
        send(chunk).start()
        total[...] += nt(scaled_ref[chunk], state_grad)

    copies[2].wait()
    out_keys_ref[...] = (total[...] + dkeys_ref[...]).astype(BF16)
    copies[3].start()
    copies[3].wait()
    for chunk in range(CHUNKS):
        send(chunk).wait()


def whole(shape):
    return pl.BlockSpec(shape, lambda i: (0,) * len(shape))


TOKENS_BY_STEP = pl.BlockSpec((TOK, WIDE), lambda i: (0, i))
ROW_BY_STEP = pl.BlockSpec((1, WIDE), lambda i: (0, i))
TOKENS_BY_LONG = pl.BlockSpec((TOK, LONG), lambda i: (0, i))
ROW_BY_LONG = pl.BlockSpec((1, LONG), lambda i: (0, i))
MAP = whole((TOK, N))
FACTORS = whole((TOK, 2 * SLICE))
COLUMNS = whole((TOK, 128))
ROWS = whole((STEPS, 2 * HPS, TOK))
ROWS_BY_STEP = pl.BlockSpec((1, 2 * HPS, TOK), lambda i: (i, 0, 0))
SUMS = whole((PARTS, 2, TOK))


def state_by(width, rows=N):
    return pl.BlockSpec((width // SLICE, rows, SLICE), lambda i: (i, 0, 0))


def shape(*dims, dtype=F32):
    return jax.ShapeDtypeStruct(dims, dtype)


def in_hbm(*dims, dtype=F32):
    return pltpu.HBM(dims, dtype)


def hbm(*arrays):
    return [pltpu.with_memory_space_constraint(a, pltpu.HBM) for a in arrays]


ANY = pl.BlockSpec(memory_space=pl.ANY)


def manual_call(kernel, name, operands, out_shape, scratch):
    return pl.pallas_call(
        kernel,
        name=name,
        in_specs=[ANY] * len(operands),
        out_specs=[ANY] * len(out_shape),
        out_shape=out_shape,
        scratch_shapes=scratch,
        compiler_params=pltpu.CompilerParams(vmem_limit_bytes=VMEM_MIB << 20),
        cost_estimate=pl.CostEstimate(flops=2**30, bytes_accessed=8 * 2**20, transcendentals=0),
    )(*operands)


def call(kernel, name, in_specs, out_specs, out_shape, scratch=(), gmacs=1.0, mib=8.0, steps=COLS // LONG):
    return pl.pallas_call(
        kernel,
        name=name,
        grid=(steps,),
        in_specs=in_specs,
        out_specs=out_specs,
        out_shape=out_shape,
        scratch_shapes=list(scratch),
        compiler_params=pltpu.CompilerParams(vmem_limit_bytes=VMEM_MIB << 20),
        cost_estimate=pl.CostEstimate(flops=int(2e9 * gmacs), bytes_accessed=int(mib * 2**20), transcendentals=0),
    )


def whole_call(kernel, name, in_specs, out_specs, out_shape):
    return pl.pallas_call(
        kernel,
        name=name,
        grid=(1,),
        in_specs=in_specs,
        out_specs=out_specs,
        out_shape=out_shape,
        compiler_params=pltpu.CompilerParams(vmem_limit_bytes=VMEM_MIB << 20),
        cost_estimate=pl.CostEstimate(flops=2**24, bytes_accessed=2**21, transcendentals=0),
    )


def exchange(a, axis):
    return lax.all_to_all(a, axis, 0, 0)


def body(inputs, gate_input, step_size, input_map, output_map, decay_rate, skip_weight, norm_gain, out_grad):
    rate = decay_rate.reshape(1, HEADS)
    gain = norm_gain.reshape(1, COLS)
    skip = jnp.repeat(skip_weight, P_SIZE).reshape(1, COLS)
    tokens = shape(TOK, COLS, dtype=BF16)
    score_scratch = [
        pltpu.VMEM((BLKS, SUB, SUB), F32),
        pltpu.VMEM((BLKS // 2, SUB, SUB), BF16),
        pltpu.VMEM((HALF, HALF), BF16),
    ]
    norm_scratch = [pltpu.VMEM((TOK, 128), F32)] * 2

    queries = output_map
    inputs, gate_input, step_size, input_map, output_map, rate, skip = hbm(
        inputs, gate_input, step_size, input_map, output_map, rate, skip
    )
    chunk_scratch = pltpu.VMEM((CHUNKS, TOK, LONG), BF16)
    dma = pltpu.SemaphoreType.DMA

    ends, factors, columns, rows = manual_call(
        ends_kernel,
        "segment_ends",
        (step_size, rate, inputs, input_map),
        [
            in_hbm(SEGS, N + TAIL, SLICE, dtype=BF16),
            in_hbm(TOK, 2 * SLICE, dtype=BF16),
            in_hbm(TOK, 128),
            in_hbm(STEPS, 2 * HPS, TOK),
        ],
        [
            pltpu.VMEM((HEADS, TOK), F32),
            pltpu.VMEM((1, HEADS), F32),
            chunk_scratch,
            pltpu.VMEM((TOK, N), BF16),
            pltpu.VMEM((SEGS, N + TAIL, SLICE), BF16),
            pltpu.VMEM((TOK, 2 * SLICE), BF16),
            pltpu.VMEM((TOK, 128), F32),
            pltpu.VMEM((STEPS, 2 * HPS, TOK), F32),
            pltpu.VMEM((N, TOK), BF16),
            dma((6,)),
            dma((CHUNKS,)),
            dma((CHUNKS,)),
        ],
    )
    all_ends = exchange(ends, "ctx")

    mixed_local, silu, scaled = call(
        local_kernel,
        "within_segment",
        [TOKENS_BY_STEP, TOKENS_BY_STEP, MAP, MAP, FACTORS, COLUMNS, ROWS_BY_STEP, ROW_BY_STEP],
        [TOKENS_BY_STEP] * 3,
        [in_hbm(TOK, COLS, dtype=BF16)] * 3,
        score_scratch,
        steps=STEPS,
        gmacs=4.0,
    )(inputs, gate_input, input_map, output_map, factors, columns, rows, skip)
    all_ends, mixed_local, silu, scaled = lax.optimization_barrier((all_ends, mixed_local, silu, scaled))

    starts = whole_call(
        forward_scan_kernel,
        "forward_scan",
        [whole((SEGS, N + TAIL, SLICE))],
        whole((SEGS, N, SLICE)),
        shape(SEGS, N, SLICE, dtype=BF16),
    )(all_ends)
    state_in = exchange(starts, "ctx")

    mixed, sums = call(
        gate_kernel,
        "carry_and_gate",
        [TOKENS_BY_LONG, state_by(LONG), MAP, FACTORS, TOKENS_BY_LONG, ROW_BY_LONG, TOKENS_BY_LONG],
        [TOKENS_BY_LONG, SUMS],
        [tokens, shape(PARTS, 2, TOK)],
        norm_scratch,
    )(mixed_local, state_in, queries, factors, silu, gain, *hbm(out_grad))
    sums = exchange(sums, "tp")

    dy, local_grads = call(
        grad_kernel,
        "local_grads",
        [TOKENS_BY_LONG, SUMS, MAP, FACTORS, TOKENS_BY_LONG, ROW_BY_LONG, TOKENS_BY_LONG],
        [TOKENS_BY_LONG, state_by(LONG)],
        [in_hbm(TOK, COLS, dtype=BF16), in_hbm(SEGS, N, SLICE, dtype=BF16)],
        norm_scratch + [pltpu.VMEM((N, TOK), BF16)],
    )(mixed, sums, queries, factors, silu, gain, out_grad)
    all_grads = exchange(local_grads, "ctx")

    normed, grad_gate = call(
        norm_kernel,
        "normed_and_gate",
        [TOKENS_BY_LONG, SUMS, TOKENS_BY_LONG, ROW_BY_LONG, TOKENS_BY_LONG],
        [TOKENS_BY_LONG, TOKENS_BY_LONG],
        [tokens, tokens],
        norm_scratch,
    )(*hbm(mixed, sums, gate_input, gain, out_grad))

    dx, dkeys, dqueries = call(
        back_kernel,
        "within_segment_back",
        [TOKENS_BY_STEP, TOKENS_BY_STEP, state_by(WIDE), MAP, MAP, FACTORS, COLUMNS, ROWS_BY_STEP, ROW_BY_STEP],
        [TOKENS_BY_STEP, MAP, MAP],
        [in_hbm(TOK, COLS, dtype=BF16), in_hbm(TOK, N), shape(TOK, N, dtype=BF16)],
        score_scratch
        + [
            pltpu.VMEM((BLKS, SUB, SUB), F32),
            pltpu.VMEM((BLKS // 2, SUB, SUB), F32),
            pltpu.VMEM((HALF, HALF), F32),
            pltpu.VMEM((TOK, N), F32),
        ],
        steps=STEPS,
        gmacs=6.0,
    )(inputs, dy, *hbm(state_in), input_map, output_map, factors, columns, rows, skip)

    grad_starts = whole_call(
        backward_scan_kernel,
        "backward_scan",
        [whole((SEGS, N, SLICE)), pl.BlockSpec((SEGS, TAIL, SLICE), lambda i: (0, N // TAIL, 0))],
        whole((SEGS, N, SLICE)),
        shape(SEGS, N, SLICE, dtype=BF16),
    )(all_grads, all_ends)
    state_grad = exchange(grad_starts, "ctx")

    grad_inputs, grad_keys = manual_call(
        final_kernel,
        "final_grads",
        (*hbm(dx, scaled), state_grad, *hbm(input_map, factors, dkeys)),
        [tokens, shape(TOK, N, dtype=BF16)],
        [
            chunk_scratch,
            chunk_scratch,
            pltpu.VMEM((SEGS, N, SLICE), BF16),
            pltpu.VMEM((TOK, N), BF16),
            pltpu.VMEM((TOK, 2 * SLICE), BF16),
            pltpu.VMEM((TOK, N), F32),
            chunk_scratch,
            pltpu.VMEM((TOK, N), BF16),
            pltpu.VMEM((TOK, N), F32),
            dma((4,)),
            dma((3, CHUNKS)),
            dma((CHUNKS,)),
        ],
    )
    return normed, grad_inputs, grad_gate, grad_keys, dqueries


def solution(mesh):
    both = P("ctx", "tp")
    return jax.shard_map(
        body,
        mesh=mesh,
        in_specs=(both, both, P("tp", "ctx"), both, both, P("tp"), P("tp"), P("tp"), both),
        out_specs=(both,) * 5,
        check_vma=False,
    )
```

```python
import jax
import jax.numpy as jnp
from jax import lax
from jax.experimental import pallas as pl
from jax.experimental.pallas import tpu as pltpu
from jax.sharding import PartitionSpec as P

H = 256
P_SIZE = 64
N = 256
EPS = 1e-05
LOG2E = 1.4426950408889634

SEGS = 16
PARTS = 8
TOK = 512
HEADS = 32
COLS = HEADS * P_SIZE
SLICE = 128
TAIL = 16
WIDE = 256
LONG = 1024
STEPS = COLS // WIDE
CHUNKS = COLS // LONG
HPS = WIDE // P_SIZE
VMEM_MIB = 36
SUB = 128
BLKS = TOK // SUB
HALF = TOK // 2

F32 = jnp.float32
BF16 = jnp.bfloat16
END, START, MIDDLE, QUARTER = range(4)


def nn(a, b):
    return jnp.dot(a, b, preferred_element_type=F32)


def nt(a, b):
    return lax.dot_general(a, b, (((1,), (1,)), ((), ())), preferred_element_type=F32)


def transposed(a):
    return a.astype(F32).T.astype(a.dtype)


def split(a):
    high = a.astype(BF16)
    return high, (a - high.astype(F32)).astype(BF16)


def expand(factors, which, step, width):
    row = lax.broadcasted_iota(jnp.int32, (2 * SLICE, width), 0)
    head = (lax.broadcasted_iota(jnp.int32, (2 * SLICE, width), 1) >> 6) + (width // P_SIZE) * step
    pick = jnp.where((row & 127) == head + HEADS * which, 1.0, 0.0).astype(BF16)
    return nn(factors, pick)


def two_heads(a):
    lane = lax.broadcasted_iota(jnp.int32, a.shape, 1)
    zero = jnp.zeros_like(a)
    return jnp.concatenate([jnp.where(lane < P_SIZE, a, zero), jnp.where(lane < P_SIZE, zero, a)], 0)


def blk(i):
    return slice(i * SUB, (i + 1) * SUB)


def columns_of(array, chunk):
    return array.at[:, pl.ds(pl.multiple_of(chunk * LONG, LONG), LONG)]


def slices_of(array, chunk):
    return array.at[pl.ds(chunk * (LONG // SLICE), LONG // SLICE)]


def ends_kernel(
    step_in, rate_in, x_in, keys_in, out, fac_out, col_out, row_out,
    step_ref, rate_ref, x_ref, keys_ref, ends_ref, fac_ref, col_ref, row_ref, keys_t, small, come, go,
):
    def fetch(chunk):
        return pltpu.make_async_copy(columns_of(x_in, chunk), x_ref.at[chunk], come.at[chunk])

    def send(chunk):
        return pltpu.make_async_copy(slices_of(ends_ref, chunk), slices_of(out, chunk), go.at[chunk])

    pairs = [(step_in, step_ref), (rate_in, rate_ref), (keys_in, keys_ref)]
    pairs += [(fac_ref, fac_out), (col_ref, col_out), (row_ref, row_out)]
    copies = [pltpu.make_async_copy(a, b, small.at[i]) for i, (a, b) in enumerate(pairs)]
    for copy in copies[:3]:
        copy.start()
    for chunk in range(CHUNKS):
        fetch(chunk).start()
    copies[0].wait()
    copies[1].wait()

    steps = step_ref[...]
    diagonal = lax.broadcasted_iota(jnp.int32, (HEADS, HEADS), 0) == lax.broadcasted_iota(jnp.int32, (HEADS, HEADS), 1)
    rate = jnp.sum(jnp.where(diagonal, rate_ref[...], 0.0), axis=1, keepdims=True)
    logs = steps * (rate * -LOG2E)
    high = logs.astype(BF16)
    rest = logs - high.astype(F32)
    mid, low = split(rest)
    source = lax.broadcasted_iota(jnp.int32, (TOK, TOK), 0)
    target = lax.broadcasted_iota(jnp.int32, (TOK, TOK), 1)
    upper = jnp.where(source <= target, 1.0, 0.0).astype(BF16)
    sums = nn(jnp.concatenate([high.astype(F32), mid.astype(F32), low.astype(F32)], 0).astype(BF16), upper)
    cum = sums[:HEADS] + sums[HEADS : 2 * HEADS] + sums[2 * HEADS :]
    shifted = cum - jnp.log(steps) * LOG2E
    token = lax.broadcasted_iota(jnp.int32, (HEADS, TOK), 1)
    one = jnp.ones_like(steps)
    end = jnp.exp2(cum[:, TOK - 1 :] - cum) * steps
    start = jnp.exp2(cum)
    middle = jnp.exp2(-jnp.abs(cum - cum[:, HALF - 1 : HALF])) * jnp.where(token < HALF, steps, one)
    near = jnp.where(token < HALF, cum[:, SUB - 1 : SUB], cum[:, 3 * SUB - 1 : 3 * SUB])
    quarter = jnp.exp2(-jnp.abs(cum - near)) * jnp.where((token & SUB) == 0, steps, one)
    high, low = split(jnp.concatenate([end, start, middle, quarter], 0).T)
    fac_ref[:, :128] = high
    fac_ref[:, 128:] = low
    copies[3].start()
    copies[2].wait()
    keys_t[...] = transposed(keys_ref[...])

    @pl.loop(0, CHUNKS)
    def _(chunk):
        fetch(chunk).wait()
        factor = expand(fac_ref[...], END, chunk, LONG)
        ends = nn(keys_t[...], (x_ref[chunk].astype(F32) * factor).astype(BF16)).astype(BF16)
        head = (lax.broadcasted_iota(jnp.int32, (HEADS, LONG), 1) >> 6) + LONG // P_SIZE * chunk
        own = lax.broadcasted_iota(jnp.int32, (HEADS, LONG), 0) == head
        decay = jnp.sum(jnp.where(own, start[:, TOK - 1 :], 0.0), axis=0, keepdims=True)
        decay = jnp.broadcast_to(decay, (TAIL, LONG)).astype(BF16)
        for part in range(LONG // SLICE):
            lanes = slice(part * SLICE, (part + 1) * SLICE)
            ends_ref[chunk * (LONG // SLICE) + part, :N] = ends[:, lanes]
            ends_ref[chunk * (LONG // SLICE) + part, N:] = decay[:, lanes]
        send(chunk).start()

    col_ref[...] = jnp.concatenate([cum, shifted, cum, shifted], 0).T
    for part in range(STEPS):
        heads = slice(part * HPS, (part + 1) * HPS)
        row_ref[part] = jnp.concatenate([cum[heads], shifted[heads]], 0)
    copies[4].start()
    copies[5].start()
    for copy in copies[3:]:
        copy.wait()
    for chunk in range(CHUNKS):
        send(chunk).wait()


def weights(col, row, scores):
    return (jnp.exp2(jnp.minimum(col - row, 0.0)) * scores).astype(BF16)


def local_kernel(
    x_ref, gate_ref, keys_ref, queries_ref, fac_ref, col_ref, row_ref, skip_ref,
    out_ref, gated_ref, ratio_ref, scaled_ref, near, off1, off2,
):
    step = pl.program_id(0)

    @pl.when(step == 0)
    def _():
        target = lax.broadcasted_iota(jnp.int32, (SUB, SUB), 0)
        source = lax.broadcasted_iota(jnp.int32, (SUB, SUB), 1)
        for i in range(BLKS):
            scores = nt(queries_ref[blk(i)], keys_ref[blk(i)])
            near[i] = jnp.where(source <= target, scores, 0.0)
        for i in range(BLKS // 2):
            off1[i] = nt(queries_ref[blk(2 * i + 1)], keys_ref[blk(2 * i)]).astype(BF16)
        off2[...] = nt(queries_ref[HALF:], keys_ref[:HALF]).astype(BF16)

    factors = fac_ref[...]
    x = x_ref[...]
    wide = x.astype(F32)
    middle = expand(factors, MIDDLE, step, WIDE)
    quarter = expand(factors, QUARTER, step, WIDE)
    cols = pltpu.roll(col_ref[...], lax.rem(128 - HPS * step, 128), 1)
    scaled_ref[...] = (wide * expand(factors, END, step, WIDE)).astype(BF16)
    gate = gate_ref[...].astype(F32)
    silu = gate * jax.nn.sigmoid(gate)
    ratio_ref[...] = (silu * expand(factors, START, step, WIDE)).astype(BF16)
    far = nn(off2[...], (wide[:HALF] * middle[:HALF]).astype(BF16)) * middle[HALF:]
    skip = skip_ref[...] * wide
    for i in range(BLKS):
        total = skip[blk(i)]
        if i % 2:
            before = (wide[blk(i - 1)] * quarter[blk(i - 1)]).astype(BF16)
            total += nn(off1[i // 2], before) * quarter[blk(i)]
        if i >= 2:
            total += far[blk(i - 2)]
        scores = near[i]
        for pair in range(WIDE // SLICE):
            lanes = slice(pair * SLICE, (pair + 1) * SLICE)
            both = []
            for j in (2 * pair, 2 * pair + 1):
                row = row_ref[0, HPS + j : HPS + j + 1, blk(i)]
                both.append(weights(cols[blk(i), j : j + 1], row, scores))
            within = nn(jnp.concatenate(both, 1), two_heads(x[blk(i), lanes]))
            mixed = total[:, lanes] + within
            out_ref[blk(i), lanes] = mixed.astype(BF16)
            gated_ref[blk(i), lanes] = (mixed * silu[blk(i), lanes]).astype(BF16)


def forward_scan_kernel(in_ref, out_ref):
    running = jnp.zeros((N, SLICE), F32)
    for k in range(SEGS):
        out_ref[k] = running.astype(BF16)
        decay = in_ref[k, N : N + TAIL][:1].astype(F32)
        running = running * decay + in_ref[k, :N].astype(F32)


def backward_scan_kernel(in_ref, ends_in, out, out_ref, decay_ref, sems):
    decays = pltpu.make_async_copy(ends_in.at[:, pl.ds(N, TAIL)], decay_ref, sems.at[SEGS])
    decays.start()
    sends = [pltpu.make_async_copy(out_ref.at[k], out.at[k], sems.at[k]) for k in range(SEGS)]
    running = jnp.zeros((N, SLICE), F32)
    decays.wait()
    for k in reversed(range(SEGS)):
        out_ref[k] = running.astype(BF16)
        sends[k].start()
        running = running * decay_ref[k][:1].astype(F32) + in_ref[k].astype(F32)
    for send in sends:
        send.wait()


def state_of(ref):
    return jnp.concatenate([ref[part] for part in range(ref.shape[0])], 1)


def fold(a):
    total = a[:, :128]
    for lane in range(128, a.shape[1], 128):
        total += a[:, lane : lane + 128]
    return total


def chunk_lanes(chunk):
    return pl.ds(pl.multiple_of(chunk * LONG, LONG), LONG)


def state_chunk(ref, chunk):
    first = chunk * (LONG // SLICE)
    return jnp.concatenate([ref[first + part] for part in range(LONG // SLICE)], 1)


def gate_kernel(
    local_ref, state_ref, queries_ref, ratio_ref, gain_ref, grad_in, gated_ref, sums_ref,
    grad_ref, square, product, come,
):
    def fetch(chunk):
        return pltpu.make_async_copy(columns_of(grad_in, chunk), grad_ref.at[chunk], come.at[chunk])

    for chunk in range(CHUNKS):
        fetch(chunk).start()
    square[...] = jnp.zeros_like(square)
    product[...] = jnp.zeros_like(product)

    @pl.loop(0, CHUNKS)
    def _(chunk):
        lanes = chunk_lanes(chunk)
        carried = nn(queries_ref[...], state_chunk(state_ref, chunk))
        gated = local_ref[:, lanes].astype(F32) + ratio_ref[:, lanes].astype(F32) * carried
        gated_ref[:, lanes] = gated.astype(BF16)
        square[...] += fold(gated * gated)
        fetch(chunk).wait()
        product[...] += fold(gated * (gain_ref[:, lanes] * grad_ref[chunk].astype(F32)))

    both = jnp.concatenate(
        [jnp.sum(square[...].T, axis=0, keepdims=True), jnp.sum(product[...].T, axis=0, keepdims=True)], 0
    )
    for part in range(PARTS):
        sums_ref[part] = both


def norm_terms(sums_ref, inverse, slope):
    total = sums_ref[0]
    for part in range(1, PARTS):
        total += sums_ref[part]
    inv_rms = lax.rsqrt(total[:1] / (H * P_SIZE) + EPS)
    ratio = inv_rms * inv_rms * inv_rms * total[1:] / (H * P_SIZE)
    inverse[...] = jnp.broadcast_to(inv_rms, (128, TOK)).T
    slope[...] = jnp.broadcast_to(ratio, (128, TOK)).T


def wide_of(ref):
    return jnp.concatenate([ref[...]] * (LONG // 128), 1)


def grad_kernel(
    gated_ref, sums_ref, queries_ref, ratio_ref, gain_ref, grad_ref, out,
    local_ref, inverse, slope, go,
):
    def send(chunk):
        return pltpu.make_async_copy(slices_of(local_ref, chunk), slices_of(out, chunk), go.at[chunk])

    norm_terms(sums_ref, inverse, slope)
    queries_t = transposed(queries_ref[...])

    @pl.loop(0, CHUNKS, unroll=True)
    def _(chunk):
        lanes = chunk_lanes(chunk)
        gated = gated_ref[:, lanes].astype(F32)
        grad_gated = wide_of(inverse) * (gain_ref[:, lanes] * grad_ref[:, lanes].astype(F32)) - gated * wide_of(slope)
        weighted = (grad_gated * ratio_ref[:, lanes].astype(F32)).astype(BF16)
        local = nn(queries_t, weighted).astype(BF16)
        for part in range(LONG // SLICE):
            local_ref[chunk * (LONG // SLICE) + part] = local[:, part * SLICE : (part + 1) * SLICE]
        send(chunk).start()

    for chunk in range(CHUNKS):
        send(chunk).wait()


def norm_kernel(
    local_ref, sums_ref, gate_ref, gain_ref, grad_ref, state_ref, queries_ref, fac_ref,
    normed_ref, out_ref, dy_ref, dq_ref, inverse, slope,
):
    step = pl.program_id(0)

    @pl.when(step == 0)
    def _():
        norm_terms(sums_ref, inverse, slope)
        dq_ref[...] = jnp.zeros_like(dq_ref)

    gate = gate_ref[...].astype(F32)
    sig = jax.nn.sigmoid(gate)
    state = state_of(state_ref)
    start = expand(fac_ref[...], START, step, LONG)
    mixed = local_ref[...].astype(F32) + nn(queries_ref[...], state) * start
    silu = gate * sig
    gated = mixed * silu
    gain = wide_of(inverse) * gain_ref[...]
    normed_ref[...] = (gated * gain).astype(BF16)
    grad_gated = gain * grad_ref[...].astype(F32) - gated * wide_of(slope)
    out_ref[...] = (grad_gated * mixed * (sig * (1.0 + gate * (1.0 - sig)))).astype(BF16)
    dy = grad_gated * silu
    dy_ref[...] = dy.astype(BF16)
    dq_ref[...] += nt((dy * start).astype(BF16), state)


def back_kernel(
    x_ref, dy_ref, dq_ref, keys_ref, queries_ref, fac_ref, col_ref, row_ref, skip_ref,
    dx_ref, dkeys_ref, dqueries_ref,
    near, off1, off2, dnear, doff1, doff2, dq,
):
    step = pl.program_id(0)

    @pl.when(step == 0)
    def _():
        source = lax.broadcasted_iota(jnp.int32, (SUB, SUB), 0)
        target = lax.broadcasted_iota(jnp.int32, (SUB, SUB), 1)
        for i in range(BLKS):
            scores = nt(keys_ref[blk(i)], queries_ref[blk(i)])
            near[i] = jnp.where(source <= target, scores, 0.0)
        for i in range(BLKS // 2):
            off1[i] = nt(keys_ref[blk(2 * i)], queries_ref[blk(2 * i + 1)]).astype(BF16)
        off2[...] = nt(keys_ref[:HALF], queries_ref[HALF:]).astype(BF16)
        dnear[...] = jnp.zeros_like(dnear)
        doff1[...] = jnp.zeros_like(doff1)
        doff2[...] = jnp.zeros_like(doff2)
        dq[...] = dq_ref[...]

    factors = fac_ref[...]
    x = x_ref[...]
    wide = x.astype(F32)
    dy = dy_ref[...]
    dwide = dy.astype(F32)
    middle = expand(factors, MIDDLE, step, WIDE)
    quarter = expand(factors, QUARTER, step, WIDE)
    cols = pltpu.roll(col_ref[...], lax.rem(128 - HPS * step, 128), 1)
    above = (wide[:HALF] * middle[:HALF]).astype(BF16)
    below = (dwide[HALF:] * middle[HALF:]).astype(BF16)
    far = nn(off2[...], below) * middle[:HALF]
    doff2[...] += nt(above, below)
    skip = skip_ref[...] * dwide
    for i in range(BLKS):
        total = skip[blk(i)]
        if i % 2 == 0:
            above = (wide[blk(i)] * quarter[blk(i)]).astype(BF16)
            below = (dwide[blk(i + 1)] * quarter[blk(i + 1)]).astype(BF16)
            total += nn(off1[i // 2], below) * quarter[blk(i)]
            doff1[i // 2] += nt(above, below)
        if i < 2:
            total += far[blk(i)]
        scores = near[i]
        dscores = dnear[i]
        for pair in range(WIDE // SLICE):
            lanes = slice(pair * SLICE, (pair + 1) * SLICE)
            dy_two = two_heads(dy[blk(i), lanes])
            dweights = nt(x[blk(i), lanes], dy_two)
            both = []
            for place, j in enumerate((2 * pair, 2 * pair + 1)):
                row = row_ref[0, j : j + 1, blk(i)]
                decay = jnp.exp2(jnp.minimum(row - cols[blk(i), HEADS + j : HEADS + j + 1], 0.0))
                both.append((decay * scores).astype(BF16))
                dscores += decay * dweights[:, place * SUB : (place + 1) * SUB]
            dx_ref[blk(i), lanes] = (total[:, lanes] + nn(jnp.concatenate(both, 1), dy_two)).astype(BF16)
        dnear[i] = dscores

    @pl.when(step == STEPS - 1)
    def _():
        source = lax.broadcasted_iota(jnp.int32, (SUB, SUB), 0)
        target = lax.broadcasted_iota(jnp.int32, (SUB, SUB), 1)
        last = doff2[...]
        dkeys_ref[...] = jnp.zeros_like(dkeys_ref)
        dkeys_ref[:HALF] += nn(last.astype(BF16), queries_ref[HALF:])
        dq[HALF:] += nn(last.T.astype(BF16), keys_ref[:HALF])
        for i in range(BLKS // 2):
            part = doff1[i]
            dkeys_ref[blk(2 * i)] += nn(part.astype(BF16), queries_ref[blk(2 * i + 1)])
            dq[blk(2 * i + 1)] += nn(part.T.astype(BF16), keys_ref[blk(2 * i)])
        for i in range(BLKS):
            part = jnp.where(source <= target, dnear[i], 0.0)
            dkeys_ref[blk(i)] += nn(part.astype(BF16), queries_ref[blk(i)])
            dq[blk(i)] += nn(part.T.astype(BF16), keys_ref[blk(i)])
        dqueries_ref[...] = dq[...].astype(BF16)


def final_kernel(
    dx_in, scaled_in, grad_ref, keys_in, fac_in, dkeys_in, out, out_keys,
    dx_ref, scaled_ref, keys_ref, fac_ref, dkeys_ref, out_ref, out_keys_ref, total, small, come, go,
):
    def fetch(chunk):
        return (
            pltpu.make_async_copy(columns_of(scaled_in, chunk), scaled_ref.at[chunk], come.at[0, chunk]),
            pltpu.make_async_copy(columns_of(dx_in, chunk), dx_ref.at[chunk], come.at[1, chunk]),
        )

    def send(chunk):
        return pltpu.make_async_copy(out_ref.at[chunk], columns_of(out, chunk), go.at[chunk])

    pairs = [(keys_in, keys_ref), (fac_in, fac_ref), (dkeys_in, dkeys_ref), (out_keys_ref, out_keys)]
    copies = [pltpu.make_async_copy(a, b, small.at[i]) for i, (a, b) in enumerate(pairs)]
    copies[0].start()
    copies[1].start()
    for chunk in range(CHUNKS):
        for copy in fetch(chunk):
            copy.start()
    copies[2].start()
    total[...] = jnp.zeros_like(total)
    copies[0].wait()
    copies[1].wait()

    @pl.loop(0, CHUNKS)
    def _(chunk):
        for copy in fetch(chunk):
            copy.wait()
        state_grad = state_chunk(grad_ref, chunk)
        from_end = nn(keys_ref[...], state_grad) * expand(fac_ref[...], END, chunk, LONG)
        out_ref[chunk] = (dx_ref[chunk].astype(F32) + from_end).astype(BF16)
        send(chunk).start()
        total[...] += nt(scaled_ref[chunk], state_grad)

    copies[2].wait()
    out_keys_ref[...] = (total[...] + dkeys_ref[...]).astype(BF16)
    copies[3].start()
    copies[3].wait()
    for chunk in range(CHUNKS):
        send(chunk).wait()


def whole(shape):
    return pl.BlockSpec(shape, lambda i: (0,) * len(shape))


TOKENS_BY_STEP = pl.BlockSpec((TOK, WIDE), lambda i: (0, i))
ROW_BY_STEP = pl.BlockSpec((1, WIDE), lambda i: (0, i))
TOKENS_BY_LONG = pl.BlockSpec((TOK, LONG), lambda i: (0, i))
ROW_BY_LONG = pl.BlockSpec((1, LONG), lambda i: (0, i))
MAP = whole((TOK, N))
FACTORS = whole((TOK, 2 * SLICE))
COLUMNS = whole((TOK, 128))
ROWS = whole((STEPS, 2 * HPS, TOK))
ROWS_BY_STEP = pl.BlockSpec((1, 2 * HPS, TOK), lambda i: (i, 0, 0))
SUMS = whole((PARTS, 2, TOK))


def state_by(width, rows=N):
    return pl.BlockSpec((width // SLICE, rows, SLICE), lambda i: (i, 0, 0))


def shape(*dims, dtype=F32):
    return jax.ShapeDtypeStruct(dims, dtype)


def in_hbm(*dims, dtype=F32):
    return pltpu.HBM(dims, dtype)


def hbm(*arrays):
    return [pltpu.with_memory_space_constraint(a, pltpu.HBM) for a in arrays]


ANY = pl.BlockSpec(memory_space=pl.ANY)


HERE = pl.BlockSpec(memory_space=pltpu.VMEM)


def manual_call(kernel, name, operands, out_shape, scratch, here=(), out_here=()):
    return pl.pallas_call(
        kernel,
        name=name,
        in_specs=[HERE if i in here else ANY for i in range(len(operands))],
        out_specs=[HERE if i in out_here else ANY for i in range(len(out_shape))],
        out_shape=out_shape,
        scratch_shapes=scratch,
        compiler_params=pltpu.CompilerParams(vmem_limit_bytes=VMEM_MIB << 20),
        cost_estimate=pl.CostEstimate(flops=2**30, bytes_accessed=8 * 2**20, transcendentals=0),
    )(*operands)


def call(kernel, name, in_specs, out_specs, out_shape, scratch=(), gmacs=1.0, mib=8.0, steps=COLS // LONG):
    return pl.pallas_call(
        kernel,
        name=name,
        grid=(steps,),
        in_specs=in_specs,
        out_specs=out_specs,
        out_shape=out_shape,
        scratch_shapes=list(scratch),
        compiler_params=pltpu.CompilerParams(vmem_limit_bytes=VMEM_MIB << 20),
        cost_estimate=pl.CostEstimate(flops=int(2e9 * gmacs), bytes_accessed=int(mib * 2**20), transcendentals=0),
    )


def exchange(a, axis):
    return lax.all_to_all(a, axis, 0, 0)


def body(inputs, gate_input, step_size, input_map, output_map, decay_rate, skip_weight, norm_gain, out_grad):
    rate = decay_rate.reshape(1, HEADS)
    gain = norm_gain.reshape(1, COLS)
    skip = jnp.repeat(skip_weight, P_SIZE).reshape(1, COLS)
    tokens = shape(TOK, COLS, dtype=BF16)
    score_scratch = [
        pltpu.VMEM((BLKS, SUB, SUB), F32),
        pltpu.VMEM((BLKS // 2, SUB, SUB), BF16),
        pltpu.VMEM((HALF, HALF), BF16),
    ]
    norm_scratch = [pltpu.VMEM((TOK, 128), F32)] * 2

    queries = output_map
    inputs, gate_input, step_size, input_map, output_map, rate, skip = hbm(
        inputs, gate_input, step_size, input_map, output_map, rate, skip
    )
    chunk_scratch = pltpu.VMEM((CHUNKS, TOK, LONG), BF16)
    dma = pltpu.SemaphoreType.DMA

    ends, factors, columns, rows = manual_call(
        ends_kernel,
        "segment_ends",
        (step_size, rate, inputs, input_map),
        [
            in_hbm(SEGS, N + TAIL, SLICE, dtype=BF16),
            in_hbm(TOK, 2 * SLICE, dtype=BF16),
            in_hbm(TOK, 128),
            in_hbm(STEPS, 2 * HPS, TOK),
        ],
        [
            pltpu.VMEM((HEADS, TOK), F32),
            pltpu.VMEM((1, HEADS), F32),
            chunk_scratch,
            pltpu.VMEM((TOK, N), BF16),
            pltpu.VMEM((SEGS, N + TAIL, SLICE), BF16),
            pltpu.VMEM((TOK, 2 * SLICE), BF16),
            pltpu.VMEM((TOK, 128), F32),
            pltpu.VMEM((STEPS, 2 * HPS, TOK), F32),
            pltpu.VMEM((N, TOK), BF16),
            dma((6,)),
            dma((CHUNKS,)),
            dma((CHUNKS,)),
        ],
    )
    all_ends = exchange(ends, "ctx")

    mixed_local, gated_local, ratio, scaled = call(
        local_kernel,
        "within_segment",
        [TOKENS_BY_STEP, TOKENS_BY_STEP, MAP, MAP, FACTORS, COLUMNS, ROWS_BY_STEP, ROW_BY_STEP],
        [TOKENS_BY_STEP] * 4,
        [in_hbm(TOK, COLS, dtype=BF16)] * 4,
        score_scratch,
        steps=STEPS,
        gmacs=4.0,
    )(inputs, gate_input, input_map, output_map, factors, columns, rows, skip)
    all_ends, mixed_local, gated_local, ratio, scaled = lax.optimization_barrier(
        (all_ends, mixed_local, gated_local, ratio, scaled)
    )

    (starts,) = manual_call(
        forward_scan_kernel, "forward_scan", (all_ends,), [shape(SEGS, N, SLICE, dtype=BF16)], [], (0,), (0,)
    )
    state_in = exchange(starts, "ctx")

    gated, sums = manual_call(
        gate_kernel,
        "carry_and_gate",
        (gated_local, state_in, queries, ratio, gain, *hbm(out_grad)),
        [tokens, shape(PARTS, 2, TOK)],
        [chunk_scratch] + norm_scratch + [dma((CHUNKS,))],
        here=range(5),
        out_here=range(2),
    )
    sums = exchange(sums, "tp")

    (local_grads,) = manual_call(
        grad_kernel,
        "local_grads",
        (gated, sums, queries, ratio, gain, out_grad),
        [in_hbm(SEGS, N, SLICE, dtype=BF16)],
        [pltpu.VMEM((SEGS, N, SLICE), BF16)] + norm_scratch + [dma((CHUNKS,))],
        here=range(6),
    )
    all_grads = exchange(local_grads, "ctx")

    normed, grad_gate, dy, dq = call(
        norm_kernel,
        "normed_and_gate",
        [TOKENS_BY_LONG, SUMS, TOKENS_BY_LONG, ROW_BY_LONG, TOKENS_BY_LONG, state_by(LONG), MAP, FACTORS],
        [TOKENS_BY_LONG, TOKENS_BY_LONG, TOKENS_BY_LONG, MAP],
        [tokens, tokens, in_hbm(TOK, COLS, dtype=BF16), in_hbm(TOK, N)],
        norm_scratch,
        gmacs=2.0,
    )(*hbm(mixed_local, sums, gate_input, gain, out_grad, state_in, output_map, factors))

    dx, dkeys, dqueries = call(
        back_kernel,
        "within_segment_back",
        [TOKENS_BY_STEP, TOKENS_BY_STEP, MAP, MAP, MAP, FACTORS, COLUMNS, ROWS_BY_STEP, ROW_BY_STEP],
        [TOKENS_BY_STEP, MAP, MAP],
        [in_hbm(TOK, COLS, dtype=BF16), in_hbm(TOK, N), shape(TOK, N, dtype=BF16)],
        score_scratch
        + [
            pltpu.VMEM((BLKS, SUB, SUB), F32),
            pltpu.VMEM((BLKS // 2, SUB, SUB), F32),
            pltpu.VMEM((HALF, HALF), F32),
            pltpu.VMEM((TOK, N), F32),
        ],
        steps=STEPS,
        gmacs=6.0,
    )(inputs, *hbm(dy, dq), input_map, output_map, factors, columns, rows, skip)

    (grad_starts,) = manual_call(
        backward_scan_kernel,
        "backward_scan",
        (all_grads, all_ends),
        [in_hbm(SEGS, N, SLICE, dtype=BF16)],
        [pltpu.VMEM((SEGS, N, SLICE), BF16), pltpu.VMEM((SEGS, TAIL, SLICE), BF16), dma((SEGS + 1,))],
        here=(0,),
    )
    state_grad = exchange(grad_starts, "ctx")

    grad_inputs, grad_keys = manual_call(
        final_kernel,
        "final_grads",
        (*hbm(dx, scaled), state_grad, *hbm(input_map, factors, dkeys)),
        [tokens, shape(TOK, N, dtype=BF16)],
        [
            chunk_scratch,
            chunk_scratch,
            pltpu.VMEM((TOK, N), BF16),
            pltpu.VMEM((TOK, 2 * SLICE), BF16),
            pltpu.VMEM((TOK, N), F32),
            chunk_scratch,
            pltpu.VMEM((TOK, N), BF16),
            pltpu.VMEM((TOK, N), F32),
            dma((4,)),
            dma((2, CHUNKS)),
            dma((CHUNKS,)),
        ],
        here=(2,),
    )
    return normed, grad_inputs, grad_gate, grad_keys, dqueries


def solution(mesh):
    both = P("ctx", "tp")
    return jax.shard_map(
        body,
        mesh=mesh,
        in_specs=(both, both, P("tp", "ctx"), both, both, P("tp"), P("tp"), P("tp"), both),
        out_specs=(both,) * 5,
        check_vma=False,
    )
```

```python
import functools

import jax
import jax.numpy as jnp
from jax import lax
from jax.experimental import pallas as pl
from jax.experimental.pallas import tpu as pltpu
from jax.sharding import PartitionSpec as P

H = 256
P_SIZE = 64
N = 256
EPS = 1e-05
LOG2E = 1.4426950408889634

SEGS = 16
PARTS = 8
TOK = 512
HEADS = 32
COLS = HEADS * P_SIZE
SLICE = 128
TAIL = 16
WIDE = 256
LONG = 1024
STEPS = COLS // WIDE
CHUNKS = COLS // LONG
HPS = WIDE // P_SIZE
VMEM_MIB = 36
NORM = 512
NORM_CHUNKS = COLS // NORM
EARLY_STEPS = 2
EARLY_CHUNKS = 1
SUB = 128
BLKS = TOK // SUB
HALF = TOK // 2

F32 = jnp.float32
BF16 = jnp.bfloat16
END, START, MIDDLE, QUARTER = range(4)


def nn(a, b):
    return jnp.dot(a, b, preferred_element_type=F32)


def nt(a, b):
    return lax.dot_general(a, b, (((1,), (1,)), ((), ())), preferred_element_type=F32)


def transposed(a):
    return a.astype(F32).T.astype(a.dtype)


def split(a):
    high = a.astype(BF16)
    return high, (a - high.astype(F32)).astype(BF16)


def expand(factors, which, step, width):
    row = lax.broadcasted_iota(jnp.int32, (2 * SLICE, width), 0)
    head = (lax.broadcasted_iota(jnp.int32, (2 * SLICE, width), 1) >> 6) + (width // P_SIZE) * step
    pick = jnp.where((row & 127) == head + HEADS * which, 1.0, 0.0).astype(BF16)
    return nn(factors, pick)


def two_heads(a):
    lane = lax.broadcasted_iota(jnp.int32, a.shape, 1)
    zero = jnp.zeros_like(a)
    return jnp.concatenate([jnp.where(lane < P_SIZE, a, zero), jnp.where(lane < P_SIZE, zero, a)], 0)


def column_of(row_ref):
    place = lax.broadcasted_iota(jnp.int32, (HEADS, HEADS), 0)
    diagonal = place == lax.broadcasted_iota(jnp.int32, (HEADS, HEADS), 1)
    return jnp.sum(jnp.where(diagonal, row_ref[...], 0.0), axis=1, keepdims=True)


def channel_row(column, step):
    head = (lax.broadcasted_iota(jnp.int32, (HEADS, WIDE), 1) >> 6) + HPS * step
    own = lax.broadcasted_iota(jnp.int32, (HEADS, WIDE), 0) == head
    return jnp.sum(jnp.where(own, column, 0.0), axis=0, keepdims=True)


def blk(i):
    return slice(i * SUB, (i + 1) * SUB)


def columns_of(array, chunk):
    return array.at[:, pl.ds(pl.multiple_of(chunk * LONG, LONG), LONG)]


def slices_of(array, chunk):
    return array.at[pl.ds(chunk * (LONG // SLICE), LONG // SLICE)]


def ends_kernel(
    step_in, rate_in, x_in, keys_in, out, fac_out, col_out, row_out,
    step_ref, rate_ref, x_ref, keys_ref, ends_ref, fac_ref, col_ref, row_ref, keys_t, small, come, go,
):
    def fetch(chunk):
        return pltpu.make_async_copy(columns_of(x_in, chunk), x_ref.at[chunk], come.at[chunk])

    def send(chunk):
        return pltpu.make_async_copy(slices_of(ends_ref, chunk), slices_of(out, chunk), go.at[chunk])

    pairs = [(step_in, step_ref), (rate_in, rate_ref), (keys_in, keys_ref)]
    pairs += [(fac_ref, fac_out), (col_ref, col_out), (row_ref, row_out)]
    copies = [pltpu.make_async_copy(a, b, small.at[i]) for i, (a, b) in enumerate(pairs)]
    for copy in copies[:3]:
        copy.start()
    for chunk in range(CHUNKS):
        fetch(chunk).start()
    copies[0].wait()
    copies[1].wait()

    steps = step_ref[...]
    logs = steps * (column_of(rate_ref) * -LOG2E)
    high = logs.astype(BF16)
    rest = logs - high.astype(F32)
    mid, low = split(rest)
    source = lax.broadcasted_iota(jnp.int32, (TOK, TOK), 0)
    target = lax.broadcasted_iota(jnp.int32, (TOK, TOK), 1)
    upper = jnp.where(source <= target, 1.0, 0.0).astype(BF16)
    sums = nn(jnp.concatenate([high.astype(F32), mid.astype(F32), low.astype(F32)], 0).astype(BF16), upper)
    cum = sums[:HEADS] + sums[HEADS : 2 * HEADS] + sums[2 * HEADS :]
    shifted = cum - jnp.log(steps) * LOG2E
    token = lax.broadcasted_iota(jnp.int32, (HEADS, TOK), 1)
    one = jnp.ones_like(steps)
    end = jnp.exp2(cum[:, TOK - 1 :] - cum) * steps
    start = jnp.exp2(cum)
    middle = jnp.exp2(-jnp.abs(cum - cum[:, HALF - 1 : HALF])) * jnp.where(token < HALF, steps, one)
    near = jnp.where(token < HALF, cum[:, SUB - 1 : SUB], cum[:, 3 * SUB - 1 : 3 * SUB])
    quarter = jnp.exp2(-jnp.abs(cum - near)) * jnp.where((token & SUB) == 0, steps, one)
    high, low = split(jnp.concatenate([end, start, middle, quarter], 0).T)
    fac_ref[:, :128] = high
    fac_ref[:, 128:] = low
    copies[3].start()
    copies[2].wait()
    keys_t[...] = transposed(keys_ref[...])

    @pl.loop(0, CHUNKS)
    def _(chunk):
        fetch(chunk).wait()
        factor = expand(fac_ref[...], END, chunk, LONG)
        ends = nn(keys_t[...], (x_ref[chunk].astype(F32) * factor).astype(BF16)).astype(BF16)
        head = (lax.broadcasted_iota(jnp.int32, (HEADS, LONG), 1) >> 6) + LONG // P_SIZE * chunk
        own = lax.broadcasted_iota(jnp.int32, (HEADS, LONG), 0) == head
        decay = jnp.sum(jnp.where(own, start[:, TOK - 1 :], 0.0), axis=0, keepdims=True)
        decay = jnp.broadcast_to(decay, (TAIL, LONG)).astype(BF16)
        for part in range(LONG // SLICE):
            lanes = slice(part * SLICE, (part + 1) * SLICE)
            ends_ref[chunk * (LONG // SLICE) + part, :N] = ends[:, lanes]
            ends_ref[chunk * (LONG // SLICE) + part, N:] = decay[:, lanes]
        send(chunk).start()

    col_ref[...] = jnp.concatenate([cum, shifted, cum, shifted], 0).T
    for part in range(STEPS):
        heads = slice(part * HPS, (part + 1) * HPS)
        row_ref[part] = jnp.concatenate([cum[heads], shifted[heads]], 0)
    copies[4].start()
    copies[5].start()
    for copy in copies[3:]:
        copy.wait()
    for chunk in range(CHUNKS):
        send(chunk).wait()


def weights(col, row, scores):
    return (jnp.exp2(jnp.minimum(col - row, 0.0)) * scores).astype(BF16)


def steps_of(array, step):
    return array.at[:, pl.ds(pl.multiple_of(step * WIDE, WIDE), WIDE)]


def bounds(part, early, total):
    count = early * (1 - lax.axis_index("tp") % 2)
    return (0, count) if part == 0 else (count, total)


def local_kernel(part, x_in, gate_in, *refs):
    small_in, refs = refs[:6], refs[6:]
    outs, refs = refs[-19:-15], refs[-15:]
    x_buf, gate_buf, small_refs, results = refs[0], refs[1], refs[2:8], refs[8]
    near, off1, off2, small, come, go = refs[9:]
    keys_ref, queries_ref, fac_ref, col_ref, row_ref, skip_ref = small_refs
    first, last = bounds(part, EARLY_STEPS, STEPS)

    def fetch(step):
        return (
            pltpu.make_async_copy(steps_of(x_in, step), x_buf.at[step], come.at[0, step]),
            pltpu.make_async_copy(steps_of(gate_in, step), gate_buf.at[step], come.at[1, step]),
        )

    def send(step):
        return [pltpu.make_async_copy(results.at[i, step], steps_of(out, step), go.at[i, step]) for i, out in enumerate(outs)]

    @pl.when(first < last)
    def _():
        copies = [pltpu.make_async_copy(a, b, small.at[i]) for i, (a, b) in enumerate(zip(small_in, small_refs))]
        for copy in copies:
            copy.start()

        @pl.loop(first, last)
        def _(step):
            for copy in fetch(step):
                copy.start()

        for copy in copies:
            copy.wait()
        target = lax.broadcasted_iota(jnp.int32, (SUB, SUB), 0)
        source = lax.broadcasted_iota(jnp.int32, (SUB, SUB), 1)
        for i in range(BLKS):
            scores = nt(queries_ref[blk(i)], keys_ref[blk(i)])
            near[i] = jnp.where(source <= target, scores, 0.0)
        for i in range(BLKS // 2):
            off1[i] = nt(queries_ref[blk(2 * i + 1)], keys_ref[blk(2 * i)]).astype(BF16)
        off2[...] = nt(queries_ref[HALF:], keys_ref[:HALF]).astype(BF16)

        @pl.loop(first, last)
        def _(step):
            for copy in fetch(step):
                copy.wait()
            factors = fac_ref[...]
            x = x_buf[step]
            wide = x.astype(F32)
            middle = expand(factors, MIDDLE, step, WIDE)
            quarter = expand(factors, QUARTER, step, WIDE)
            cols = pltpu.roll(col_ref[...], lax.rem(128 - HPS * step, 128), 1)
            results[3, step] = (wide * expand(factors, END, step, WIDE)).astype(BF16)
            gate = gate_buf[step].astype(F32)
            silu = gate * jax.nn.sigmoid(gate)
            results[2, step] = (silu * expand(factors, START, step, WIDE)).astype(BF16)
            far = nn(off2[...], (wide[:HALF] * middle[:HALF]).astype(BF16)) * middle[HALF:]
            skip = channel_row(column_of(skip_ref), step) * wide
            for i in range(BLKS):
                total = skip[blk(i)]
                if i % 2:
                    before = (wide[blk(i - 1)] * quarter[blk(i - 1)]).astype(BF16)
                    total += nn(off1[i // 2], before) * quarter[blk(i)]
                if i >= 2:
                    total += far[blk(i - 2)]
                scores = near[i]
                for pair in range(WIDE // SLICE):
                    lanes = slice(pair * SLICE, (pair + 1) * SLICE)
                    both = []
                    for j in (2 * pair, 2 * pair + 1):
                        row = row_ref[step, HPS + j : HPS + j + 1, blk(i)]
                        both.append(weights(cols[blk(i), j : j + 1], row, scores))
                    within = nn(jnp.concatenate(both, 1), two_heads(x[blk(i), lanes]))
                    mixed = total[:, lanes] + within
                    results[0, step, blk(i), lanes] = mixed.astype(BF16)
                    results[1, step, blk(i), lanes] = (mixed * silu[blk(i), lanes]).astype(BF16)
            for copy in send(step):
                copy.start()

        @pl.loop(first, last)
        def _(step):
            for copy in send(step):
                copy.wait()


def forward_scan_kernel(in_ref, out_ref):
    running = jnp.zeros((N, SLICE), F32)
    for k in range(SEGS):
        out_ref[k] = running.astype(BF16)
        decay = in_ref[k, N : N + TAIL][:1].astype(F32)
        running = running * decay + in_ref[k, :N].astype(F32)


def backward_scan_kernel(in_ref, ends_in, out, out_ref, decay_ref, sems):
    decays = pltpu.make_async_copy(ends_in.at[:, pl.ds(N, TAIL)], decay_ref, sems.at[SEGS])
    decays.start()
    sends = [pltpu.make_async_copy(out_ref.at[k], out.at[k], sems.at[k]) for k in range(SEGS)]
    running = jnp.zeros((N, SLICE), F32)
    decays.wait()
    for k in reversed(range(SEGS)):
        out_ref[k] = running.astype(BF16)
        sends[k].start()
        running = running * decay_ref[k][:1].astype(F32) + in_ref[k].astype(F32)
    for send in sends:
        send.wait()


def state_of(ref):
    return jnp.concatenate([ref[part] for part in range(ref.shape[0])], 1)


def fold(a):
    total = a[:, :128]
    for lane in range(128, a.shape[1], 128):
        total += a[:, lane : lane + 128]
    return total


def chunk_lanes(chunk):
    return pl.ds(pl.multiple_of(chunk * LONG, LONG), LONG)


def state_chunk(ref, chunk):
    first = chunk * (LONG // SLICE)
    return jnp.concatenate([ref[first + part] for part in range(LONG // SLICE)], 1)


def gate_kernel(
    local_ref, state_ref, queries_ref, ratio_ref, gain_ref, grad_in, gated_ref, sums_ref,
    grad_ref, square, product, come,
):
    def fetch(chunk):
        return pltpu.make_async_copy(columns_of(grad_in, chunk), grad_ref.at[chunk], come.at[chunk])

    for chunk in range(CHUNKS):
        fetch(chunk).start()
    square[...] = jnp.zeros_like(square)
    product[...] = jnp.zeros_like(product)

    @pl.loop(0, CHUNKS)
    def _(chunk):
        lanes = chunk_lanes(chunk)
        carried = nn(queries_ref[...], state_chunk(state_ref, chunk))
        gated = local_ref[:, lanes].astype(F32) + ratio_ref[:, lanes].astype(F32) * carried
        gated_ref[:, lanes] = gated.astype(BF16)
        square[...] += fold(gated * gated)

    @pl.loop(0, CHUNKS)
    def _(chunk):
        lanes = chunk_lanes(chunk)
        fetch(chunk).wait()
        product[...] += fold(gated_ref[:, lanes].astype(F32) * (gain_ref[:, lanes] * grad_ref[chunk].astype(F32)))

    both = jnp.concatenate(
        [jnp.sum(square[...].T, axis=0, keepdims=True), jnp.sum(product[...].T, axis=0, keepdims=True)], 0
    )
    for part in range(PARTS):
        sums_ref[part] = both


def norm_terms(sums_ref, inverse, slope):
    total = sums_ref[0]
    for part in range(1, PARTS):
        total += sums_ref[part]
    inv_rms = lax.rsqrt(total[:1] / (H * P_SIZE) + EPS)
    ratio = inv_rms * inv_rms * inv_rms * total[1:] / (H * P_SIZE)
    inverse[...] = jnp.broadcast_to(inv_rms, (128, TOK)).T
    slope[...] = jnp.broadcast_to(ratio, (128, TOK)).T


def wide_of(ref, width=LONG):
    return jnp.concatenate([ref[...]] * (width // 128), 1)


def grad_kernel(
    gated_ref, sums_ref, queries_ref, ratio_ref, gain_ref, grad_ref, out,
    local_ref, inverse, slope, go,
):
    def send(chunk):
        return pltpu.make_async_copy(slices_of(local_ref, chunk), slices_of(out, chunk), go.at[chunk])

    norm_terms(sums_ref, inverse, slope)
    queries_t = transposed(queries_ref[...])

    @pl.loop(0, CHUNKS, unroll=True)
    def _(chunk):
        lanes = chunk_lanes(chunk)
        gated = gated_ref[:, lanes].astype(F32)
        grad_gated = wide_of(inverse) * (gain_ref[:, lanes] * grad_ref[:, lanes].astype(F32)) - gated * wide_of(slope)
        weighted = (grad_gated * ratio_ref[:, lanes].astype(F32)).astype(BF16)
        local = nn(queries_t, weighted).astype(BF16)
        for part in range(LONG // SLICE):
            local_ref[chunk * (LONG // SLICE) + part] = local[:, part * SLICE : (part + 1) * SLICE]
        send(chunk).start()

    for chunk in range(CHUNKS):
        send(chunk).wait()


def norm_columns(array, chunk):
    return array.at[:, pl.ds(pl.multiple_of(chunk * NORM, NORM), NORM)]


def norm_kernel(part, local_in, gate_in, grad_in, *refs):
    small_in, refs = refs[:5], refs[5:]
    dq_in = refs[3]
    outs, dq_out, refs = refs[-16:-13], refs[-13], refs[-12:]
    bufs, small_refs, dq_ref, results = refs[0], refs[1:6], refs[6], refs[7]
    inverse, slope, small, come = refs[8:]
    sums_ref, gain_ref, state_ref, queries_ref, fac_ref = small_refs
    first, last = bounds(part, EARLY_CHUNKS, NORM_CHUNKS)

    def fetch(chunk):
        return [
            pltpu.make_async_copy(norm_columns(a, chunk), bufs.at[i, chunk], come.at[i, chunk])
            for i, a in enumerate((local_in, gate_in, grad_in))
        ]

    def send(chunk):
        return [
            pltpu.make_async_copy(results.at[i, chunk], norm_columns(out, chunk), come.at[3 + i, chunk])
            for i, out in enumerate(outs)
        ]

    @pl.when(first < last)
    def _():
        copies = [pltpu.make_async_copy(a, b, small.at[i]) for i, (a, b) in enumerate(zip(small_in, small_refs))]
        for copy in copies:
            copy.start()

        @pl.loop(first, last)
        def _(chunk):
            for copy in fetch(chunk):
                copy.start()

        for copy in copies:
            copy.wait()

        dq_ref[...] = jnp.zeros_like(dq_ref)

        @pl.when(first > 0)
        def _():
            earlier = pltpu.make_async_copy(dq_in, dq_ref, small.at[5])
            earlier.start()
            earlier.wait()

        norm_terms(sums_ref, inverse, slope)

        @pl.loop(first, last)
        def _(chunk):
            for copy in fetch(chunk):
                copy.wait()
            gate = bufs[1, chunk].astype(F32)
            sig = jax.nn.sigmoid(gate)
            parts = NORM // SLICE
            state = jnp.concatenate([state_ref[chunk * parts + i] for i in range(parts)], 1)
            start = expand(fac_ref[...], START, chunk, NORM)
            mixed = bufs[0, chunk].astype(F32) + nn(queries_ref[...], state) * start
            silu = gate * sig
            gated = mixed * silu
            gain = wide_of(inverse, NORM) * gain_ref[:, pl.ds(pl.multiple_of(chunk * NORM, NORM), NORM)]
            results[0, chunk] = (gated * gain).astype(BF16)
            grad_gated = gain * bufs[2, chunk].astype(F32) - gated * wide_of(slope, NORM)
            results[1, chunk] = (grad_gated * mixed * (sig * (1.0 + gate * (1.0 - sig)))).astype(BF16)
            dy = grad_gated * silu
            results[2, chunk] = dy.astype(BF16)
            dq_ref[...] += nt((dy * start).astype(BF16), state)
            for copy in send(chunk):
                copy.start()

        final = pltpu.make_async_copy(dq_ref, dq_out, small.at[6])
        final.start()

        @pl.loop(first, last)
        def _(chunk):
            for copy in send(chunk):
                copy.wait()

        final.wait()


def back_kernel(
    x_ref, dy_ref, dq_ref, keys_ref, queries_ref, fac_ref, col_ref, row_ref, skip_ref,
    dx_ref, dkeys_ref, dqueries_ref,
    near, off1, off2, dnear, doff1, doff2, dq,
):
    step = pl.program_id(0)

    @pl.when(step == 0)
    def _():
        source = lax.broadcasted_iota(jnp.int32, (SUB, SUB), 0)
        target = lax.broadcasted_iota(jnp.int32, (SUB, SUB), 1)
        for i in range(BLKS):
            scores = nt(keys_ref[blk(i)], queries_ref[blk(i)])
            near[i] = jnp.where(source <= target, scores, 0.0)
        for i in range(BLKS // 2):
            off1[i] = nt(keys_ref[blk(2 * i)], queries_ref[blk(2 * i + 1)]).astype(BF16)
        off2[...] = nt(keys_ref[:HALF], queries_ref[HALF:]).astype(BF16)
        dnear[...] = jnp.zeros_like(dnear)
        doff1[...] = jnp.zeros_like(doff1)
        doff2[...] = jnp.zeros_like(doff2)
        dq[...] = dq_ref[...]

    factors = fac_ref[...]
    x = x_ref[...]
    wide = x.astype(F32)
    dy = dy_ref[...]
    dwide = dy.astype(F32)
    middle = expand(factors, MIDDLE, step, WIDE)
    quarter = expand(factors, QUARTER, step, WIDE)
    cols = pltpu.roll(col_ref[...], lax.rem(128 - HPS * step, 128), 1)
    above = (wide[:HALF] * middle[:HALF]).astype(BF16)
    below = (dwide[HALF:] * middle[HALF:]).astype(BF16)
    far = nn(off2[...], below) * middle[:HALF]
    doff2[...] += nt(above, below)
    skip = channel_row(column_of(skip_ref), step) * dwide
    for i in range(BLKS):
        total = skip[blk(i)]
        if i % 2 == 0:
            above = (wide[blk(i)] * quarter[blk(i)]).astype(BF16)
            below = (dwide[blk(i + 1)] * quarter[blk(i + 1)]).astype(BF16)
            total += nn(off1[i // 2], below) * quarter[blk(i)]
            doff1[i // 2] += nt(above, below)
        if i < 2:
            total += far[blk(i)]
        scores = near[i]
        dscores = dnear[i]
        for pair in range(WIDE // SLICE):
            lanes = slice(pair * SLICE, (pair + 1) * SLICE)
            dy_two = two_heads(dy[blk(i), lanes])
            dweights = nt(x[blk(i), lanes], dy_two)
            both = []
            for place, j in enumerate((2 * pair, 2 * pair + 1)):
                row = row_ref[0, j : j + 1, blk(i)]
                decay = jnp.exp2(jnp.minimum(row - cols[blk(i), HEADS + j : HEADS + j + 1], 0.0))
                both.append((decay * scores).astype(BF16))
                dscores += decay * dweights[:, place * SUB : (place + 1) * SUB]
            dx_ref[blk(i), lanes] = (total[:, lanes] + nn(jnp.concatenate(both, 1), dy_two)).astype(BF16)
        dnear[i] = dscores

    @pl.when(step == STEPS - 1)
    def _():
        source = lax.broadcasted_iota(jnp.int32, (SUB, SUB), 0)
        target = lax.broadcasted_iota(jnp.int32, (SUB, SUB), 1)
        last = doff2[...]
        dkeys_ref[...] = jnp.zeros_like(dkeys_ref)
        dkeys_ref[:HALF] += nn(last.astype(BF16), queries_ref[HALF:])
        dq[HALF:] += nn(last.T.astype(BF16), keys_ref[:HALF])
        for i in range(BLKS // 2):
            part = doff1[i]
            dkeys_ref[blk(2 * i)] += nn(part.astype(BF16), queries_ref[blk(2 * i + 1)])
            dq[blk(2 * i + 1)] += nn(part.T.astype(BF16), keys_ref[blk(2 * i)])
        for i in range(BLKS):
            part = jnp.where(source <= target, dnear[i], 0.0)
            dkeys_ref[blk(i)] += nn(part.astype(BF16), queries_ref[blk(i)])
            dq[blk(i)] += nn(part.T.astype(BF16), keys_ref[blk(i)])
        dqueries_ref[...] = dq[...].astype(BF16)


def final_kernel(
    dx_in, scaled_in, grad_ref, keys_in, fac_in, dkeys_in, out, out_keys,
    dx_ref, scaled_ref, keys_ref, fac_ref, dkeys_ref, out_ref, out_keys_ref, total, small, come, go,
):
    def fetch(chunk):
        return (
            pltpu.make_async_copy(columns_of(scaled_in, chunk), scaled_ref.at[chunk], come.at[0, chunk]),
            pltpu.make_async_copy(columns_of(dx_in, chunk), dx_ref.at[chunk], come.at[1, chunk]),
        )

    def send(chunk):
        return pltpu.make_async_copy(out_ref.at[chunk], columns_of(out, chunk), go.at[chunk])

    pairs = [(keys_in, keys_ref), (fac_in, fac_ref), (dkeys_in, dkeys_ref), (out_keys_ref, out_keys)]
    copies = [pltpu.make_async_copy(a, b, small.at[i]) for i, (a, b) in enumerate(pairs)]
    copies[0].start()
    copies[1].start()
    for chunk in range(CHUNKS):
        for copy in fetch(chunk):
            copy.start()
    copies[2].start()
    total[...] = jnp.zeros_like(total)
    copies[0].wait()
    copies[1].wait()

    @pl.loop(0, CHUNKS)
    def _(chunk):
        for copy in fetch(chunk):
            copy.wait()
        state_grad = state_chunk(grad_ref, chunk)
        from_end = nn(keys_ref[...], state_grad) * expand(fac_ref[...], END, chunk, LONG)
        out_ref[chunk] = (dx_ref[chunk].astype(F32) + from_end).astype(BF16)
        send(chunk).start()
        total[...] += nt(scaled_ref[chunk], state_grad)

    copies[2].wait()
    out_keys_ref[...] = (total[...] + dkeys_ref[...]).astype(BF16)
    copies[3].start()
    copies[3].wait()
    for chunk in range(CHUNKS):
        send(chunk).wait()


def whole(shape):
    return pl.BlockSpec(shape, lambda i: (0,) * len(shape))


TOKENS_BY_STEP = pl.BlockSpec((TOK, WIDE), lambda i: (0, i))
ROW_BY_STEP = pl.BlockSpec((1, WIDE), lambda i: (0, i))
TOKENS_BY_LONG = pl.BlockSpec((TOK, LONG), lambda i: (0, i))
ROW_BY_LONG = pl.BlockSpec((1, LONG), lambda i: (0, i))
MAP = whole((TOK, N))
FACTORS = whole((TOK, 2 * SLICE))
COLUMNS = whole((TOK, 128))
ROWS = whole((STEPS, 2 * HPS, TOK))
ROWS_BY_STEP = pl.BlockSpec((1, 2 * HPS, TOK), lambda i: (i, 0, 0))
SUMS = whole((PARTS, 2, TOK))


def state_by(width, rows=N):
    return pl.BlockSpec((width // SLICE, rows, SLICE), lambda i: (i, 0, 0))


def shape(*dims, dtype=F32):
    return jax.ShapeDtypeStruct(dims, dtype)


def in_hbm(*dims, dtype=F32):
    return pltpu.HBM(dims, dtype)


def hbm(*arrays):
    return [pltpu.with_memory_space_constraint(a, pltpu.HBM) for a in arrays]


ANY = pl.BlockSpec(memory_space=pl.ANY)


HERE = pl.BlockSpec(memory_space=pltpu.VMEM)


def manual_call(kernel, name, operands, out_shape, scratch, here=(), out_here=()):
    return pl.pallas_call(
        kernel,
        name=name,
        in_specs=[HERE if i in here else ANY for i in range(len(operands))],
        out_specs=[HERE if i in out_here else ANY for i in range(len(out_shape))],
        out_shape=out_shape,
        scratch_shapes=scratch,
        compiler_params=pltpu.CompilerParams(vmem_limit_bytes=VMEM_MIB << 20),
        cost_estimate=pl.CostEstimate(flops=2**30, bytes_accessed=8 * 2**20, transcendentals=0),
    )(*operands)


def call(kernel, name, in_specs, out_specs, out_shape, scratch=(), gmacs=1.0, mib=8.0, steps=COLS // LONG):
    return pl.pallas_call(
        kernel,
        name=name,
        grid=(steps,),
        in_specs=in_specs,
        out_specs=out_specs,
        out_shape=out_shape,
        scratch_shapes=list(scratch),
        compiler_params=pltpu.CompilerParams(vmem_limit_bytes=VMEM_MIB << 20),
        cost_estimate=pl.CostEstimate(flops=int(2e9 * gmacs), bytes_accessed=int(mib * 2**20), transcendentals=0),
    )


def split_call(kernel, name, here_first, operands, out_shape, scratch, limit, gmacs):
    def call_part(part, given):
        return pl.pallas_call(
            functools.partial(kernel, part),
            name=name,
            in_specs=[ANY] * (len(operands) + len(given)),
            out_specs=[ANY] * len(out_shape),
            out_shape=out_shape,
            input_output_aliases={len(operands) + i: i for i in range(len(given))},
            scratch_shapes=scratch,
            compiler_params=pltpu.CompilerParams(vmem_limit_bytes=limit << 20),
            cost_estimate=pl.CostEstimate(flops=int(2e9 * gmacs), bytes_accessed=12 * 2**20, transcendentals=0),
        )(*operands, *given)

    before = call_part(0, [])
    here, *before = lax.optimization_barrier((here_first, *before))
    return here, lambda: call_part(1, before)


def exchange(a, axis):
    return lax.all_to_all(a, axis, 0, 0)


def body(inputs, gate_input, step_size, input_map, output_map, decay_rate, skip_weight, norm_gain, out_grad):
    rate = decay_rate.reshape(1, HEADS)
    gain = norm_gain.reshape(1, COLS)
    skip = skip_weight.reshape(1, HEADS)
    tokens = shape(TOK, COLS, dtype=BF16)
    score_scratch = [
        pltpu.VMEM((BLKS, SUB, SUB), F32),
        pltpu.VMEM((BLKS // 2, SUB, SUB), BF16),
        pltpu.VMEM((HALF, HALF), BF16),
    ]
    norm_scratch = [pltpu.VMEM((TOK, 128), F32)] * 2

    queries = output_map
    inputs, gate_input, step_size, input_map, output_map, rate, skip = hbm(
        inputs, gate_input, step_size, input_map, output_map, rate, skip
    )
    chunk_scratch = pltpu.VMEM((CHUNKS, TOK, LONG), BF16)
    dma = pltpu.SemaphoreType.DMA

    ends, factors, columns, rows = manual_call(
        ends_kernel,
        "segment_ends",
        (step_size, rate, inputs, input_map),
        [
            in_hbm(SEGS, N + TAIL, SLICE, dtype=BF16),
            in_hbm(TOK, 2 * SLICE, dtype=BF16),
            in_hbm(TOK, 128),
            in_hbm(STEPS, 2 * HPS, TOK),
        ],
        [
            pltpu.VMEM((HEADS, TOK), F32),
            pltpu.VMEM((1, HEADS), F32),
            chunk_scratch,
            pltpu.VMEM((TOK, N), BF16),
            pltpu.VMEM((SEGS, N + TAIL, SLICE), BF16),
            pltpu.VMEM((TOK, 2 * SLICE), BF16),
            pltpu.VMEM((TOK, 128), F32),
            pltpu.VMEM((STEPS, 2 * HPS, TOK), F32),
            pltpu.VMEM((N, TOK), BF16),
            dma((6,)),
            dma((CHUNKS,)),
            dma((CHUNKS,)),
        ],
    )
    score_steps = pltpu.VMEM((STEPS, TOK, WIDE), BF16)
    ends, rest = split_call(
        local_kernel,
        "within_segment",
        ends,
        hbm(inputs, gate_input, input_map, output_map, factors, columns, rows, skip),
        [in_hbm(TOK, COLS, dtype=BF16)] * 4,
        [
            score_steps,
            score_steps,
            pltpu.VMEM((TOK, N), BF16),
            pltpu.VMEM((TOK, N), BF16),
            pltpu.VMEM((TOK, 2 * SLICE), BF16),
            pltpu.VMEM((TOK, 128), F32),
            pltpu.VMEM((STEPS, 2 * HPS, TOK), F32),
            pltpu.VMEM((1, HEADS), F32),
            pltpu.VMEM((4, STEPS, TOK, WIDE), BF16),
            *score_scratch,
            dma((6,)),
            dma((2, STEPS)),
            dma((4, STEPS)),
        ],
        40,
        4.0,
    )
    all_ends = exchange(ends, "ctx")
    mixed_local, gated_local, ratio, scaled = rest()
    all_ends, mixed_local, gated_local, ratio, scaled = lax.optimization_barrier(
        (all_ends, mixed_local, gated_local, ratio, scaled)
    )

    (starts,) = manual_call(
        forward_scan_kernel, "forward_scan", (all_ends,), [shape(SEGS, N, SLICE, dtype=BF16)], [], (0,), (0,)
    )
    state_in = exchange(starts, "ctx")

    gated, sums = manual_call(
        gate_kernel,
        "carry_and_gate",
        (gated_local, state_in, queries, ratio, gain, *hbm(out_grad)),
        [tokens, shape(PARTS, 2, TOK)],
        [chunk_scratch] + norm_scratch + [dma((CHUNKS,))],
        here=range(5),
        out_here=range(2),
    )
    sums = exchange(sums, "tp")

    (local_grads,) = manual_call(
        grad_kernel,
        "local_grads",
        (gated, sums, queries, ratio, gain, out_grad),
        [in_hbm(SEGS, N, SLICE, dtype=BF16)],
        [pltpu.VMEM((SEGS, N, SLICE), BF16)] + norm_scratch + [dma((CHUNKS,))],
        here=range(6),
    )
    local_grads, rest = split_call(
        norm_kernel,
        "normed_and_gate",
        local_grads,
        hbm(mixed_local, gate_input, out_grad, sums, gain, state_in, output_map, factors),
        [in_hbm(TOK, COLS, dtype=BF16)] * 3 + [in_hbm(TOK, N)],
        [
            pltpu.VMEM((3, NORM_CHUNKS, TOK, NORM), BF16),
            pltpu.VMEM((PARTS, 2, TOK), F32),
            pltpu.VMEM((1, COLS), F32),
            pltpu.VMEM((SEGS, N, SLICE), BF16),
            pltpu.VMEM((TOK, N), BF16),
            pltpu.VMEM((TOK, 2 * SLICE), BF16),
            pltpu.VMEM((TOK, N), F32),
            pltpu.VMEM((3, NORM_CHUNKS, TOK, NORM), BF16),
            *norm_scratch,
            dma((7,)),
            dma((6, NORM_CHUNKS)),
        ],
        48,
        2.0,
    )
    all_grads = exchange(local_grads, "ctx")
    normed, grad_gate, dy, dq = rest()

    dx, dkeys, dqueries = call(
        back_kernel,
        "within_segment_back",
        [TOKENS_BY_STEP, TOKENS_BY_STEP, MAP, MAP, MAP, FACTORS, COLUMNS, ROWS_BY_STEP, whole((1, HEADS))],
        [TOKENS_BY_STEP, MAP, MAP],
        [in_hbm(TOK, COLS, dtype=BF16), in_hbm(TOK, N), shape(TOK, N, dtype=BF16)],
        score_scratch
        + [
            pltpu.VMEM((BLKS, SUB, SUB), F32),
            pltpu.VMEM((BLKS // 2, SUB, SUB), F32),
            pltpu.VMEM((HALF, HALF), F32),
            pltpu.VMEM((TOK, N), F32),
        ],
        steps=STEPS,
        gmacs=6.0,
    )(inputs, *hbm(dy, dq), input_map, output_map, factors, columns, rows, skip)

    (grad_starts,) = manual_call(
        backward_scan_kernel,
        "backward_scan",
        (all_grads, all_ends),
        [in_hbm(SEGS, N, SLICE, dtype=BF16)],
        [pltpu.VMEM((SEGS, N, SLICE), BF16), pltpu.VMEM((SEGS, TAIL, SLICE), BF16), dma((SEGS + 1,))],
        here=(0,),
    )
    state_grad = exchange(grad_starts, "ctx")

    grad_inputs, grad_keys = manual_call(
        final_kernel,
        "final_grads",
        (*hbm(dx, scaled), state_grad, *hbm(input_map, factors, dkeys)),
        [tokens, shape(TOK, N, dtype=BF16)],
        [
            chunk_scratch,
            chunk_scratch,
            pltpu.VMEM((TOK, N), BF16),
            pltpu.VMEM((TOK, 2 * SLICE), BF16),
            pltpu.VMEM((TOK, N), F32),
            chunk_scratch,
            pltpu.VMEM((TOK, N), BF16),
            pltpu.VMEM((TOK, N), F32),
            dma((4,)),
            dma((2, CHUNKS)),
            dma((CHUNKS,)),
        ],
        here=(2,),
    )
    return normed, grad_inputs, grad_gate, grad_keys, dqueries


def solution(mesh):
    both = P("ctx", "tp")
    return jax.shard_map(
        body,
        mesh=mesh,
        in_specs=(both, both, P("tp", "ctx"), both, both, P("tp"), P("tp"), P("tp"), both),
        out_specs=(both,) * 5,
        check_vma=False,
    )
```

```python
import functools

import jax
import jax.numpy as jnp
from jax import lax
from jax.experimental import pallas as pl
from jax.experimental.pallas import tpu as pltpu
from jax.sharding import PartitionSpec as P

H = 256
P_SIZE = 64
N = 256
EPS = 1e-05
LOG2E = 1.4426950408889634

SEGS = 16
PARTS = 8
TOK = 512
HEADS = 32
COLS = HEADS * P_SIZE
SLICE = 128
TAIL = 16
WIDE = 512
LONG = 1024
STEPS = COLS // WIDE
CHUNKS = COLS // LONG
HPS = WIDE // P_SIZE
VMEM_MIB = 36
NORM = 512
NORM_CHUNKS = COLS // NORM
EARLY_STEPS = 1
EARLY_CHUNKS = 1
SUB = 128
BLKS = TOK // SUB
HALF = TOK // 2

F32 = jnp.float32
BF16 = jnp.bfloat16
END, START, MIDDLE, QUARTER = range(4)


def nn(a, b):
    return jnp.dot(a, b, preferred_element_type=F32)


def nt(a, b):
    return lax.dot_general(a, b, (((1,), (1,)), ((), ())), preferred_element_type=F32)


def transposed(a):
    return a.astype(F32).T.astype(a.dtype)


def split(a):
    high = a.astype(BF16)
    return high, (a - high.astype(F32)).astype(BF16)


def expand(factors, which, step, width):
    row = lax.broadcasted_iota(jnp.int32, (2 * SLICE, width), 0)
    head = (lax.broadcasted_iota(jnp.int32, (2 * SLICE, width), 1) >> 6) + (width // P_SIZE) * step
    pick = jnp.where((row & 127) == head + HEADS * which, 1.0, 0.0).astype(BF16)
    return nn(factors, pick)


def two_heads(a):
    lane = lax.broadcasted_iota(jnp.int32, a.shape, 1)
    zero = jnp.zeros_like(a)
    return jnp.concatenate([jnp.where(lane < P_SIZE, a, zero), jnp.where(lane < P_SIZE, zero, a)], 0)


def column_of(row_ref):
    place = lax.broadcasted_iota(jnp.int32, (HEADS, HEADS), 0)
    diagonal = place == lax.broadcasted_iota(jnp.int32, (HEADS, HEADS), 1)
    return jnp.sum(jnp.where(diagonal, row_ref[...], 0.0), axis=1, keepdims=True)


def channel_row(column, step):
    head = (lax.broadcasted_iota(jnp.int32, (HEADS, WIDE), 1) >> 6) + HPS * step
    own = lax.broadcasted_iota(jnp.int32, (HEADS, WIDE), 0) == head
    return jnp.sum(jnp.where(own, column, 0.0), axis=0, keepdims=True)


def blk(i):
    return slice(i * SUB, (i + 1) * SUB)


def columns_of(array, chunk):
    return array.at[:, pl.ds(pl.multiple_of(chunk * LONG, LONG), LONG)]


def slices_of(array, chunk):
    return array.at[pl.ds(chunk * (LONG // SLICE), LONG // SLICE)]


def ends_kernel(
    step_in, rate_in, x_in, keys_in, out, fac_out, col_out, row_out,
    step_ref, rate_ref, x_ref, keys_ref, ends_ref, fac_ref, col_ref, row_ref, keys_t, small, come, go,
):
    def fetch(chunk):
        return pltpu.make_async_copy(columns_of(x_in, chunk), x_ref.at[chunk], come.at[chunk])

    def send(chunk):
        return pltpu.make_async_copy(slices_of(ends_ref, chunk), slices_of(out, chunk), go.at[chunk])

    pairs = [(step_in, step_ref), (rate_in, rate_ref), (keys_in, keys_ref)]
    pairs += [(fac_ref, fac_out), (col_ref, col_out), (row_ref, row_out)]
    copies = [pltpu.make_async_copy(a, b, small.at[i]) for i, (a, b) in enumerate(pairs)]
    for copy in copies[:3]:
        copy.start()
    for chunk in range(CHUNKS):
        fetch(chunk).start()
    copies[0].wait()
    copies[1].wait()

    steps = step_ref[...]
    logs = steps * (column_of(rate_ref) * -LOG2E)
    high = logs.astype(BF16)
    rest = logs - high.astype(F32)
    mid, low = split(rest)
    source = lax.broadcasted_iota(jnp.int32, (TOK, TOK), 0)
    target = lax.broadcasted_iota(jnp.int32, (TOK, TOK), 1)
    upper = jnp.where(source <= target, 1.0, 0.0).astype(BF16)
    sums = nn(jnp.concatenate([high.astype(F32), mid.astype(F32), low.astype(F32)], 0).astype(BF16), upper)
    cum = sums[:HEADS] + sums[HEADS : 2 * HEADS] + sums[2 * HEADS :]
    shifted = cum - jnp.log(steps) * LOG2E
    token = lax.broadcasted_iota(jnp.int32, (HEADS, TOK), 1)
    one = jnp.ones_like(steps)
    end = jnp.exp2(cum[:, TOK - 1 :] - cum) * steps
    start = jnp.exp2(cum)
    middle = jnp.exp2(-jnp.abs(cum - cum[:, HALF - 1 : HALF])) * jnp.where(token < HALF, steps, one)
    near = jnp.where(token < HALF, cum[:, SUB - 1 : SUB], cum[:, 3 * SUB - 1 : 3 * SUB])
    quarter = jnp.exp2(-jnp.abs(cum - near)) * jnp.where((token & SUB) == 0, steps, one)
    high, low = split(jnp.concatenate([end, start, middle, quarter], 0).T)
    fac_ref[:, :128] = high
    fac_ref[:, 128:] = low
    copies[3].start()
    copies[2].wait()
    keys_t[...] = transposed(keys_ref[...])

    @pl.loop(0, CHUNKS)
    def _(chunk):
        fetch(chunk).wait()
        factor = expand(fac_ref[...], END, chunk, LONG)
        ends = nn(keys_t[...], (x_ref[chunk].astype(F32) * factor).astype(BF16)).astype(BF16)
        head = (lax.broadcasted_iota(jnp.int32, (HEADS, LONG), 1) >> 6) + LONG // P_SIZE * chunk
        own = lax.broadcasted_iota(jnp.int32, (HEADS, LONG), 0) == head
        decay = jnp.sum(jnp.where(own, start[:, TOK - 1 :], 0.0), axis=0, keepdims=True)
        decay = jnp.broadcast_to(decay, (TAIL, LONG)).astype(BF16)
        for part in range(LONG // SLICE):
            lanes = slice(part * SLICE, (part + 1) * SLICE)
            ends_ref[chunk * (LONG // SLICE) + part, :N] = ends[:, lanes]
            ends_ref[chunk * (LONG // SLICE) + part, N:] = decay[:, lanes]
        send(chunk).start()

    col_ref[...] = jnp.concatenate([cum, shifted, cum, shifted], 0).T
    for part in range(STEPS):
        heads = slice(part * HPS, (part + 1) * HPS)
        row_ref[part] = jnp.concatenate([cum[heads], shifted[heads]], 0)
    copies[4].start()
    copies[5].start()
    for copy in copies[3:]:
        copy.wait()
    for chunk in range(CHUNKS):
        send(chunk).wait()


def weights(col, row, scores):
    return (jnp.exp2(jnp.minimum(col - row, 0.0)) * scores).astype(BF16)


def steps_of(array, step):
    return array.at[:, pl.ds(pl.multiple_of(step * WIDE, WIDE), WIDE)]


def bounds(part, early, total):
    count = early * (1 - lax.axis_index("tp") % 2)
    return (0, count) if part == 0 else (count, total)


def local_kernel(part, x_in, gate_in, *refs):
    small_in, refs = refs[:6], refs[6:]
    outs, refs = refs[-19:-15], refs[-15:]
    x_buf, gate_buf, small_refs, results = refs[0], refs[1], refs[2:8], refs[8]
    near, off1, off2, small, come, go = refs[9:]
    keys_ref, queries_ref, fac_ref, col_ref, row_ref, skip_ref = small_refs
    first, last = bounds(part, EARLY_STEPS, STEPS)

    def fetch(step):
        return (
            pltpu.make_async_copy(steps_of(x_in, step), x_buf.at[step], come.at[0, step]),
            pltpu.make_async_copy(steps_of(gate_in, step), gate_buf.at[step], come.at[1, step]),
        )

    def send(step):
        return [pltpu.make_async_copy(results.at[i, step], steps_of(out, step), go.at[i, step]) for i, out in enumerate(outs)]

    @pl.when(first < last)
    def _():
        copies = [pltpu.make_async_copy(a, b, small.at[i]) for i, (a, b) in enumerate(zip(small_in, small_refs))]
        for copy in copies:
            copy.start()

        @pl.loop(first, last)
        def _(step):
            for copy in fetch(step):
                copy.start()

        for copy in copies:
            copy.wait()
        target = lax.broadcasted_iota(jnp.int32, (SUB, SUB), 0)
        source = lax.broadcasted_iota(jnp.int32, (SUB, SUB), 1)
        for i in range(BLKS):
            scores = nt(queries_ref[blk(i)], keys_ref[blk(i)])
            near[i] = jnp.where(source <= target, scores, 0.0)
        for i in range(BLKS // 2):
            off1[i] = nt(queries_ref[blk(2 * i + 1)], keys_ref[blk(2 * i)]).astype(BF16)
        off2[...] = nt(queries_ref[HALF:], keys_ref[:HALF]).astype(BF16)

        @pl.loop(first, last)
        def _(step):
            for copy in fetch(step):
                copy.wait()
            factors = fac_ref[...]
            x = x_buf[step]
            wide = x.astype(F32)
            middle = expand(factors, MIDDLE, step, WIDE)
            quarter = expand(factors, QUARTER, step, WIDE)
            cols = pltpu.roll(col_ref[...], lax.rem(128 - HPS * step, 128), 1)
            results[3, step] = (wide * expand(factors, END, step, WIDE)).astype(BF16)
            gate = gate_buf[step].astype(F32)
            silu = gate * jax.nn.sigmoid(gate)
            results[2, step] = (silu * expand(factors, START, step, WIDE)).astype(BF16)
            far = nn(off2[...], (wide[:HALF] * middle[:HALF]).astype(BF16)) * middle[HALF:]
            skip = channel_row(column_of(skip_ref), step) * wide
            for i in range(BLKS):
                total = skip[blk(i)]
                if i % 2:
                    before = (wide[blk(i - 1)] * quarter[blk(i - 1)]).astype(BF16)
                    total += nn(off1[i // 2], before) * quarter[blk(i)]
                if i >= 2:
                    total += far[blk(i - 2)]
                scores = near[i]
                for pair in range(WIDE // SLICE):
                    lanes = slice(pair * SLICE, (pair + 1) * SLICE)
                    both = []
                    for j in (2 * pair, 2 * pair + 1):
                        row = row_ref[step, HPS + j : HPS + j + 1, blk(i)]
                        both.append(weights(cols[blk(i), j : j + 1], row, scores))
                    within = nn(jnp.concatenate(both, 1), two_heads(x[blk(i), lanes]))
                    mixed = total[:, lanes] + within
                    results[0, step, blk(i), lanes] = mixed.astype(BF16)
                    results[1, step, blk(i), lanes] = (mixed * silu[blk(i), lanes]).astype(BF16)
            for copy in send(step):
                copy.start()

        @pl.loop(first, last)
        def _(step):
            for copy in send(step):
                copy.wait()


def forward_scan_kernel(in_ref, out_ref):
    running = jnp.zeros((N, SLICE), F32)
    for k in range(SEGS):
        out_ref[k] = running.astype(BF16)
        decay = in_ref[k, N : N + TAIL][:1].astype(F32)
        running = running * decay + in_ref[k, :N].astype(F32)


def backward_scan_kernel(in_ref, ends_in, out, out_ref, decay_ref, sems):
    decays = pltpu.make_async_copy(ends_in.at[:, pl.ds(N, TAIL)], decay_ref, sems.at[SEGS])
    decays.start()
    sends = [pltpu.make_async_copy(out_ref.at[k], out.at[k], sems.at[k]) for k in range(SEGS)]
    running = jnp.zeros((N, SLICE), F32)
    decays.wait()
    for k in reversed(range(SEGS)):
        out_ref[k] = running.astype(BF16)
        sends[k].start()
        running = running * decay_ref[k][:1].astype(F32) + in_ref[k].astype(F32)
    for send in sends:
        send.wait()


def state_of(ref):
    return jnp.concatenate([ref[part] for part in range(ref.shape[0])], 1)


def fold(a):
    total = a[:, :128]
    for lane in range(128, a.shape[1], 128):
        total += a[:, lane : lane + 128]
    return total


def chunk_lanes(chunk):
    return pl.ds(pl.multiple_of(chunk * LONG, LONG), LONG)


def state_chunk(ref, chunk):
    first = chunk * (LONG // SLICE)
    return jnp.concatenate([ref[first + part] for part in range(LONG // SLICE)], 1)


def gate_kernel(
    local_ref, state_ref, queries_ref, ratio_ref, gain_ref, grad_in, gated_ref, sums_ref,
    grad_ref, square, product, come,
):
    def fetch(chunk):
        return pltpu.make_async_copy(columns_of(grad_in, chunk), grad_ref.at[chunk], come.at[chunk])

    for chunk in range(CHUNKS):
        fetch(chunk).start()
    square[...] = jnp.zeros_like(square)
    product[...] = jnp.zeros_like(product)

    @pl.loop(0, CHUNKS)
    def _(chunk):
        lanes = chunk_lanes(chunk)
        carried = nn(queries_ref[...], state_chunk(state_ref, chunk))
        gated = local_ref[:, lanes].astype(F32) + ratio_ref[:, lanes].astype(F32) * carried
        gated_ref[:, lanes] = gated.astype(BF16)
        square[...] += fold(gated * gated)

    @pl.loop(0, CHUNKS)
    def _(chunk):
        lanes = chunk_lanes(chunk)
        fetch(chunk).wait()
        product[...] += fold(gated_ref[:, lanes].astype(F32) * (gain_ref[:, lanes] * grad_ref[chunk].astype(F32)))

    both = jnp.concatenate(
        [jnp.sum(square[...].T, axis=0, keepdims=True), jnp.sum(product[...].T, axis=0, keepdims=True)], 0
    )
    for part in range(PARTS):
        sums_ref[part] = both


def norm_terms(sums_ref, inverse, slope):
    total = sums_ref[0]
    for part in range(1, PARTS):
        total += sums_ref[part]
    inv_rms = lax.rsqrt(total[:1] / (H * P_SIZE) + EPS)
    ratio = inv_rms * inv_rms * inv_rms * total[1:] / (H * P_SIZE)
    inverse[...] = jnp.broadcast_to(inv_rms, (128, TOK)).T
    slope[...] = jnp.broadcast_to(ratio, (128, TOK)).T


def wide_of(ref, width=LONG):
    return jnp.concatenate([ref[...]] * (width // 128), 1)


def grad_kernel(
    gated_ref, sums_ref, queries_ref, ratio_ref, gain_ref, grad_ref, out,
    local_ref, inverse, slope, go,
):
    def send(chunk):
        return pltpu.make_async_copy(slices_of(local_ref, chunk), slices_of(out, chunk), go.at[chunk])

    norm_terms(sums_ref, inverse, slope)
    queries_t = transposed(queries_ref[...])

    @pl.loop(0, CHUNKS, unroll=True)
    def _(chunk):
        lanes = chunk_lanes(chunk)
        gated = gated_ref[:, lanes].astype(F32)
        grad_gated = wide_of(inverse) * (gain_ref[:, lanes] * grad_ref[:, lanes].astype(F32)) - gated * wide_of(slope)
        weighted = (grad_gated * ratio_ref[:, lanes].astype(F32)).astype(BF16)
        local = nn(queries_t, weighted).astype(BF16)
        for part in range(LONG // SLICE):
            local_ref[chunk * (LONG // SLICE) + part] = local[:, part * SLICE : (part + 1) * SLICE]
        send(chunk).start()

    for chunk in range(CHUNKS):
        send(chunk).wait()


def norm_columns(array, chunk):
    return array.at[:, pl.ds(pl.multiple_of(chunk * NORM, NORM), NORM)]


def norm_kernel(part, local_in, gate_in, grad_in, *refs):
    small_in, refs = refs[:5], refs[5:]
    dq_in = refs[3]
    outs, dq_out, refs = refs[-16:-13], refs[-13], refs[-12:]
    bufs, small_refs, dq_ref, results = refs[0], refs[1:6], refs[6], refs[7]
    inverse, slope, small, come = refs[8:]
    sums_ref, gain_ref, state_ref, queries_ref, fac_ref = small_refs
    first, last = bounds(part, EARLY_CHUNKS, NORM_CHUNKS)

    def fetch(chunk):
        return [
            pltpu.make_async_copy(norm_columns(a, chunk), bufs.at[i, chunk], come.at[i, chunk])
            for i, a in enumerate((local_in, gate_in, grad_in))
        ]

    def send(chunk):
        return [
            pltpu.make_async_copy(results.at[i, chunk], norm_columns(out, chunk), come.at[3 + i, chunk])
            for i, out in enumerate(outs)
        ]

    @pl.when(first < last)
    def _():
        copies = [pltpu.make_async_copy(a, b, small.at[i]) for i, (a, b) in enumerate(zip(small_in, small_refs))]
        for copy in copies:
            copy.start()

        @pl.loop(first, last)
        def _(chunk):
            for copy in fetch(chunk):
                copy.start()

        for copy in copies:
            copy.wait()

        dq_ref[...] = jnp.zeros_like(dq_ref)

        @pl.when(first > 0)
        def _():
            earlier = pltpu.make_async_copy(dq_in, dq_ref, small.at[5])
            earlier.start()
            earlier.wait()

        norm_terms(sums_ref, inverse, slope)

        @pl.loop(first, last)
        def _(chunk):
            for copy in fetch(chunk):
                copy.wait()
            gate = bufs[1, chunk].astype(F32)
            sig = jax.nn.sigmoid(gate)
            parts = NORM // SLICE
            state = jnp.concatenate([state_ref[chunk * parts + i] for i in range(parts)], 1)
            start = expand(fac_ref[...], START, chunk, NORM)
            mixed = bufs[0, chunk].astype(F32) + nn(queries_ref[...], state) * start
            silu = gate * sig
            gated = mixed * silu
            gain = wide_of(inverse, NORM) * gain_ref[:, pl.ds(pl.multiple_of(chunk * NORM, NORM), NORM)]
            results[0, chunk] = (gated * gain).astype(BF16)
            grad_gated = gain * bufs[2, chunk].astype(F32) - gated * wide_of(slope, NORM)
            results[1, chunk] = (grad_gated * mixed * (sig * (1.0 + gate * (1.0 - sig)))).astype(BF16)
            dy = grad_gated * silu
            results[2, chunk] = dy.astype(BF16)
            dq_ref[...] += nt((dy * start).astype(BF16), state)
            for copy in send(chunk):
                copy.start()

        final = pltpu.make_async_copy(dq_ref, dq_out, small.at[6])
        final.start()

        @pl.loop(first, last)
        def _(chunk):
            for copy in send(chunk):
                copy.wait()

        final.wait()


def back_kernel(
    x_ref, dy_ref, dq_ref, keys_ref, queries_ref, fac_ref, col_ref, row_ref, skip_ref,
    dx_ref, dkeys_ref, dqueries_ref,
    near, off1, off2, dnear, doff1, doff2, dq,
):
    step = pl.program_id(0)

    @pl.when(step == 0)
    def _():
        source = lax.broadcasted_iota(jnp.int32, (SUB, SUB), 0)
        target = lax.broadcasted_iota(jnp.int32, (SUB, SUB), 1)
        for i in range(BLKS):
            scores = nt(keys_ref[blk(i)], queries_ref[blk(i)])
            near[i] = jnp.where(source <= target, scores, 0.0)
        for i in range(BLKS // 2):
            off1[i] = nt(keys_ref[blk(2 * i)], queries_ref[blk(2 * i + 1)]).astype(BF16)
        off2[...] = nt(keys_ref[:HALF], queries_ref[HALF:]).astype(BF16)
        dnear[...] = jnp.zeros_like(dnear)
        doff1[...] = jnp.zeros_like(doff1)
        doff2[...] = jnp.zeros_like(doff2)
        dq[...] = dq_ref[...]

    factors = fac_ref[...]
    x = x_ref[...]
    wide = x.astype(F32)
    dy = dy_ref[...]
    dwide = dy.astype(F32)
    middle = expand(factors, MIDDLE, step, WIDE)
    quarter = expand(factors, QUARTER, step, WIDE)
    cols = pltpu.roll(col_ref[...], lax.rem(128 - HPS * step, 128), 1)
    above = (wide[:HALF] * middle[:HALF]).astype(BF16)
    below = (dwide[HALF:] * middle[HALF:]).astype(BF16)
    far = nn(off2[...], below) * middle[:HALF]
    doff2[...] += nt(above, below)
    skip = channel_row(column_of(skip_ref), step) * dwide
    for i in range(BLKS):
        total = skip[blk(i)]
        if i % 2 == 0:
            above = (wide[blk(i)] * quarter[blk(i)]).astype(BF16)
            below = (dwide[blk(i + 1)] * quarter[blk(i + 1)]).astype(BF16)
            total += nn(off1[i // 2], below) * quarter[blk(i)]
            doff1[i // 2] += nt(above, below)
        if i < 2:
            total += far[blk(i)]
        scores = near[i]
        dscores = dnear[i]
        for pair in range(WIDE // SLICE):
            lanes = slice(pair * SLICE, (pair + 1) * SLICE)
            dy_two = two_heads(dy[blk(i), lanes])
            dweights = nt(x[blk(i), lanes], dy_two)
            both = []
            for place, j in enumerate((2 * pair, 2 * pair + 1)):
                row = row_ref[0, j : j + 1, blk(i)]
                decay = jnp.exp2(jnp.minimum(row - cols[blk(i), HEADS + j : HEADS + j + 1], 0.0))
                both.append((decay * scores).astype(BF16))
                dscores += decay * dweights[:, place * SUB : (place + 1) * SUB]
            dx_ref[blk(i), lanes] = (total[:, lanes] + nn(jnp.concatenate(both, 1), dy_two)).astype(BF16)
        dnear[i] = dscores

    @pl.when(step == STEPS - 1)
    def _():
        source = lax.broadcasted_iota(jnp.int32, (SUB, SUB), 0)
        target = lax.broadcasted_iota(jnp.int32, (SUB, SUB), 1)
        last = doff2[...]
        dkeys_ref[...] = jnp.zeros_like(dkeys_ref)
        dkeys_ref[:HALF] += nn(last.astype(BF16), queries_ref[HALF:])
        dq[HALF:] += nn(last.T.astype(BF16), keys_ref[:HALF])
        for i in range(BLKS // 2):
            part = doff1[i]
            dkeys_ref[blk(2 * i)] += nn(part.astype(BF16), queries_ref[blk(2 * i + 1)])
            dq[blk(2 * i + 1)] += nn(part.T.astype(BF16), keys_ref[blk(2 * i)])
        for i in range(BLKS):
            part = jnp.where(source <= target, dnear[i], 0.0)
            dkeys_ref[blk(i)] += nn(part.astype(BF16), queries_ref[blk(i)])
            dq[blk(i)] += nn(part.T.astype(BF16), keys_ref[blk(i)])
        dqueries_ref[...] = dq[...].astype(BF16)


def final_kernel(
    dx_in, scaled_in, grad_ref, keys_in, fac_in, dkeys_in, out, out_keys,
    dx_ref, scaled_ref, keys_ref, fac_ref, dkeys_ref, out_ref, out_keys_ref, total, small, come, go,
):
    def fetch(chunk):
        return (
            pltpu.make_async_copy(columns_of(scaled_in, chunk), scaled_ref.at[chunk], come.at[0, chunk]),
            pltpu.make_async_copy(columns_of(dx_in, chunk), dx_ref.at[chunk], come.at[1, chunk]),
        )

    def send(chunk):
        return pltpu.make_async_copy(out_ref.at[chunk], columns_of(out, chunk), go.at[chunk])

    pairs = [(keys_in, keys_ref), (fac_in, fac_ref), (dkeys_in, dkeys_ref), (out_keys_ref, out_keys)]
    copies = [pltpu.make_async_copy(a, b, small.at[i]) for i, (a, b) in enumerate(pairs)]
    copies[0].start()
    copies[1].start()
    for chunk in range(CHUNKS):
        for copy in fetch(chunk):
            copy.start()
    copies[2].start()
    total[...] = jnp.zeros_like(total)
    copies[0].wait()
    copies[1].wait()

    @pl.loop(0, CHUNKS)
    def _(chunk):
        for copy in fetch(chunk):
            copy.wait()
        state_grad = state_chunk(grad_ref, chunk)
        from_end = nn(keys_ref[...], state_grad) * expand(fac_ref[...], END, chunk, LONG)
        out_ref[chunk] = (dx_ref[chunk].astype(F32) + from_end).astype(BF16)
        send(chunk).start()
        total[...] += nt(scaled_ref[chunk], state_grad)

    copies[2].wait()
    out_keys_ref[...] = (total[...] + dkeys_ref[...]).astype(BF16)
    copies[3].start()
    copies[3].wait()
    for chunk in range(CHUNKS):
        send(chunk).wait()


def whole(shape):
    return pl.BlockSpec(shape, lambda i: (0,) * len(shape))


TOKENS_BY_STEP = pl.BlockSpec((TOK, WIDE), lambda i: (0, i))
ROW_BY_STEP = pl.BlockSpec((1, WIDE), lambda i: (0, i))
TOKENS_BY_LONG = pl.BlockSpec((TOK, LONG), lambda i: (0, i))
ROW_BY_LONG = pl.BlockSpec((1, LONG), lambda i: (0, i))
MAP = whole((TOK, N))
FACTORS = whole((TOK, 2 * SLICE))
COLUMNS = whole((TOK, 128))
ROWS = whole((STEPS, 2 * HPS, TOK))
ROWS_BY_STEP = pl.BlockSpec((1, 2 * HPS, TOK), lambda i: (i, 0, 0))
SUMS = whole((PARTS, 2, TOK))


def state_by(width, rows=N):
    return pl.BlockSpec((width // SLICE, rows, SLICE), lambda i: (i, 0, 0))


def shape(*dims, dtype=F32):
    return jax.ShapeDtypeStruct(dims, dtype)


def in_hbm(*dims, dtype=F32):
    return pltpu.HBM(dims, dtype)


def hbm(*arrays):
    return [pltpu.with_memory_space_constraint(a, pltpu.HBM) for a in arrays]


ANY = pl.BlockSpec(memory_space=pl.ANY)


HERE = pl.BlockSpec(memory_space=pltpu.VMEM)


def manual_call(kernel, name, operands, out_shape, scratch, here=(), out_here=()):
    return pl.pallas_call(
        kernel,
        name=name,
        in_specs=[HERE if i in here else ANY for i in range(len(operands))],
        out_specs=[HERE if i in out_here else ANY for i in range(len(out_shape))],
        out_shape=out_shape,
        scratch_shapes=scratch,
        compiler_params=pltpu.CompilerParams(vmem_limit_bytes=VMEM_MIB << 20),
        cost_estimate=pl.CostEstimate(flops=2**30, bytes_accessed=8 * 2**20, transcendentals=0),
    )(*operands)


def call(kernel, name, in_specs, out_specs, out_shape, scratch=(), gmacs=1.0, mib=8.0, steps=COLS // LONG):
    return pl.pallas_call(
        kernel,
        name=name,
        grid=(steps,),
        in_specs=in_specs,
        out_specs=out_specs,
        out_shape=out_shape,
        scratch_shapes=list(scratch),
        compiler_params=pltpu.CompilerParams(vmem_limit_bytes=VMEM_MIB << 20),
        cost_estimate=pl.CostEstimate(flops=int(2e9 * gmacs), bytes_accessed=int(mib * 2**20), transcendentals=0),
    )


def split_call(kernel, name, here_first, operands, out_shape, scratch, limit, gmacs):
    def call_part(part, given):
        return pl.pallas_call(
            functools.partial(kernel, part),
            name=name,
            in_specs=[ANY] * (len(operands) + len(given)),
            out_specs=[ANY] * len(out_shape),
            out_shape=out_shape,
            input_output_aliases={len(operands) + i: i for i in range(len(given))},
            scratch_shapes=scratch,
            compiler_params=pltpu.CompilerParams(vmem_limit_bytes=limit << 20),
            cost_estimate=pl.CostEstimate(flops=int(2e9 * gmacs), bytes_accessed=12 * 2**20, transcendentals=0),
        )(*operands, *given)

    before = call_part(0, [])
    here, *before = lax.optimization_barrier((here_first, *before))
    return here, lambda: call_part(1, before)


def exchange(a, axis):
    return lax.all_to_all(a, axis, 0, 0)


def body(inputs, gate_input, step_size, input_map, output_map, decay_rate, skip_weight, norm_gain, out_grad):
    rate = decay_rate.reshape(1, HEADS)
    gain = norm_gain.reshape(1, COLS)
    skip = skip_weight.reshape(1, HEADS)
    tokens = shape(TOK, COLS, dtype=BF16)
    score_scratch = [
        pltpu.VMEM((BLKS, SUB, SUB), F32),
        pltpu.VMEM((BLKS // 2, SUB, SUB), BF16),
        pltpu.VMEM((HALF, HALF), BF16),
    ]
    norm_scratch = [pltpu.VMEM((TOK, 128), F32)] * 2

    queries = output_map
    inputs, gate_input, step_size, input_map, output_map, rate, skip = hbm(
        inputs, gate_input, step_size, input_map, output_map, rate, skip
    )
    chunk_scratch = pltpu.VMEM((CHUNKS, TOK, LONG), BF16)
    dma = pltpu.SemaphoreType.DMA

    ends, factors, columns, rows = manual_call(
        ends_kernel,
        "segment_ends",
        (step_size, rate, inputs, input_map),
        [
            in_hbm(SEGS, N + TAIL, SLICE, dtype=BF16),
            in_hbm(TOK, 2 * SLICE, dtype=BF16),
            in_hbm(TOK, 128),
            in_hbm(STEPS, 2 * HPS, TOK),
        ],
        [
            pltpu.VMEM((HEADS, TOK), F32),
            pltpu.VMEM((1, HEADS), F32),
            chunk_scratch,
            pltpu.VMEM((TOK, N), BF16),
            pltpu.VMEM((SEGS, N + TAIL, SLICE), BF16),
            pltpu.VMEM((TOK, 2 * SLICE), BF16),
            pltpu.VMEM((TOK, 128), F32),
            pltpu.VMEM((STEPS, 2 * HPS, TOK), F32),
            pltpu.VMEM((N, TOK), BF16),
            dma((6,)),
            dma((CHUNKS,)),
            dma((CHUNKS,)),
        ],
    )
    score_steps = pltpu.VMEM((STEPS, TOK, WIDE), BF16)
    ends, rest = split_call(
        local_kernel,
        "within_segment",
        ends,
        hbm(inputs, gate_input, input_map, output_map, factors, columns, rows, skip),
        [in_hbm(TOK, COLS, dtype=BF16)] * 4,
        [
            score_steps,
            score_steps,
            pltpu.VMEM((TOK, N), BF16),
            pltpu.VMEM((TOK, N), BF16),
            pltpu.VMEM((TOK, 2 * SLICE), BF16),
            pltpu.VMEM((TOK, 128), F32),
            pltpu.VMEM((STEPS, 2 * HPS, TOK), F32),
            pltpu.VMEM((1, HEADS), F32),
            pltpu.VMEM((4, STEPS, TOK, WIDE), BF16),
            *score_scratch,
            dma((6,)),
            dma((2, STEPS)),
            dma((4, STEPS)),
        ],
        40,
        4.0,
    )
    all_ends = exchange(ends, "ctx")
    mixed_local, gated_local, ratio, scaled = rest()
    all_ends, mixed_local, gated_local, ratio, scaled = lax.optimization_barrier(
        (all_ends, mixed_local, gated_local, ratio, scaled)
    )

    (starts,) = manual_call(
        forward_scan_kernel, "forward_scan", (all_ends,), [shape(SEGS, N, SLICE, dtype=BF16)], [], (0,), (0,)
    )
    state_in = exchange(starts, "ctx")

    gated, sums = manual_call(
        gate_kernel,
        "carry_and_gate",
        (gated_local, state_in, queries, ratio, gain, *hbm(out_grad)),
        [tokens, shape(PARTS, 2, TOK)],
        [chunk_scratch] + norm_scratch + [dma((CHUNKS,))],
        here=range(5),
        out_here=range(2),
    )
    sums = exchange(sums, "tp")

    (local_grads,) = manual_call(
        grad_kernel,
        "local_grads",
        (gated, sums, queries, ratio, gain, out_grad),
        [in_hbm(SEGS, N, SLICE, dtype=BF16)],
        [pltpu.VMEM((SEGS, N, SLICE), BF16)] + norm_scratch + [dma((CHUNKS,))],
        here=range(6),
    )
    local_grads, rest = split_call(
        norm_kernel,
        "normed_and_gate",
        local_grads,
        hbm(mixed_local, gate_input, out_grad, sums, gain, state_in, output_map, factors),
        [in_hbm(TOK, COLS, dtype=BF16)] * 3 + [in_hbm(TOK, N)],
        [
            pltpu.VMEM((3, NORM_CHUNKS, TOK, NORM), BF16),
            pltpu.VMEM((PARTS, 2, TOK), F32),
            pltpu.VMEM((1, COLS), F32),
            pltpu.VMEM((SEGS, N, SLICE), BF16),
            pltpu.VMEM((TOK, N), BF16),
            pltpu.VMEM((TOK, 2 * SLICE), BF16),
            pltpu.VMEM((TOK, N), F32),
            pltpu.VMEM((3, NORM_CHUNKS, TOK, NORM), BF16),
            *norm_scratch,
            dma((7,)),
            dma((6, NORM_CHUNKS)),
        ],
        48,
        2.0,
    )
    all_grads = exchange(local_grads, "ctx")
    normed, grad_gate, dy, dq = rest()

    dx, dkeys, dqueries = call(
        back_kernel,
        "within_segment_back",
        [TOKENS_BY_STEP, TOKENS_BY_STEP, MAP, MAP, MAP, FACTORS, COLUMNS, ROWS_BY_STEP, whole((1, HEADS))],
        [TOKENS_BY_STEP, MAP, MAP],
        [in_hbm(TOK, COLS, dtype=BF16), in_hbm(TOK, N), shape(TOK, N, dtype=BF16)],
        score_scratch
        + [
            pltpu.VMEM((BLKS, SUB, SUB), F32),
            pltpu.VMEM((BLKS // 2, SUB, SUB), F32),
            pltpu.VMEM((HALF, HALF), F32),
            pltpu.VMEM((TOK, N), F32),
        ],
        steps=STEPS,
        gmacs=6.0,
    )(inputs, *hbm(dy, dq), input_map, output_map, factors, columns, rows, skip)

    (grad_starts,) = manual_call(
        backward_scan_kernel,
        "backward_scan",
        (all_grads, all_ends),
        [in_hbm(SEGS, N, SLICE, dtype=BF16)],
        [pltpu.VMEM((SEGS, N, SLICE), BF16), pltpu.VMEM((SEGS, TAIL, SLICE), BF16), dma((SEGS + 1,))],
        here=(0,),
    )
    state_grad = exchange(grad_starts, "ctx")

    grad_inputs, grad_keys = manual_call(
        final_kernel,
        "final_grads",
        (*hbm(dx, scaled), state_grad, *hbm(input_map, factors, dkeys)),
        [tokens, shape(TOK, N, dtype=BF16)],
        [
            chunk_scratch,
            chunk_scratch,
            pltpu.VMEM((TOK, N), BF16),
            pltpu.VMEM((TOK, 2 * SLICE), BF16),
            pltpu.VMEM((TOK, N), F32),
            chunk_scratch,
            pltpu.VMEM((TOK, N), BF16),
            pltpu.VMEM((TOK, N), F32),
            dma((4,)),
            dma((2, CHUNKS)),
            dma((CHUNKS,)),
        ],
        here=(2,),
    )
    return normed, grad_inputs, grad_gate, grad_keys, dqueries


def solution(mesh):
    both = P("ctx", "tp")
    return jax.shard_map(
        body,
        mesh=mesh,
        in_specs=(both, both, P("tp", "ctx"), both, both, P("tp"), P("tp"), P("tp"), both),
        out_specs=(both,) * 5,
        check_vma=False,
    )
```
